512 devices in a mesh: front: 16 (over y, x), rows: 32 (over z, core).
Axes of the slice: x: 4, y: 4, z: 16, core: 2. Of those that a mesh axis runs over, the one named last changes fastest.
Arguments:
- own_rows: float32 [16, 8192, 1024], P('front', 'rows'), may hold values from -6 to 6
- child_tile: float32 [16, 1024, 1024], P('front', 'rows'), as said below
- col_map: int32 [16, 1024], replicated, may hold values from 0 to 1023, each once within a row
- parent: int32 [16], replicated, may hold values from 0 to 15
- live_rows: int32 [16], replicated, may hold values from 1024 to 8192
Outputs:
- r_factor: float32 [16, 1024, 1024], P('front', 'rows')
- q_panel: float32 [16, 8192, 1024], P('front', 'rows')
The draws below stay inside these ranges and needn't reach their ends.
Inputs may be any that keep to these rules, and one draw needn't show every extreme that they name: `child_tile`: each child's tile is upper triangular with a positive diagonal.
All inputs are finite; a program needn't handle non-finite values.
Results may differ from the reference program's by a relative error of at most 0.0003.
Values sent between devices are 32-bit elements; how exact they have to be, the bound alone decides.
No kernel may reach another device: no remote copies, remote signals or barrier semaphores. Data moves between devices by JAX's collectives and lax.ppermute only.
A program may use at most 64 MiB of HBM per device.

```python
import math
import jax
import jax.numpy as jnp
import numpy as np
from jax import lax

W = 1024
FRONTS = 16
ROWS = 8192


def draw_child_tile(key, part):
    key = jax.random.fold_in(key, 1)
    first, second = jax.random.split(key)
    upper = 2.0 * jax.random.normal(first, (FRONTS, W, W), jnp.float32)
    diag = jnp.exp(jax.random.uniform(second, (FRONTS, W), jnp.float32, jnp.log(2.0), jnp.log(8.0)))
    eye = jnp.eye(W, dtype=jnp.float32)
    return jnp.triu(upper, 1) + diag[:, None, :] * eye[None]


def plant(values, key, least, top_value):
    place = [jax.random.randint(jax.random.fold_in(key, axis), (), 0, length) for axis, length in enumerate(values.shape)]
    longest = values.shape.index(max(values.shape))
    neighbour = place[:longest] + [(place[longest] + 1) % values.shape[longest]] + place[longest + 1:]
    return values.at[tuple(place)].set(least).at[tuple(neighbour)].set(top_value)


def block_levels(rng, dims, cuts, least, top_value):
    loudness = 1.0
    for dim, blocks in cuts:
        steps = jax.random.uniform(jax.random.fold_in(jax.random.fold_in(rng, 6), dim), (blocks,), jnp.float32, least / len(cuts), top_value / len(cuts))
        loudness = loudness * jnp.repeat(jnp.exp(steps), dims[dim] // blocks).reshape((-1,) + (1,) * (len(dims) - 1 - dim))
    return loudness


def cumulative_ranks(amount, skew):
    weights = [(1 << 20) // math.isqrt(grade ** skew) + 1 for grade in range(1, amount + 1)]
    deviation = 1 + sum(weights) // (1 << 30)
    return np.cumsum(np.array([max(1, weight // deviation) for weight in weights]))


def ranked_ids(own_key, extent, number_of, lean):
    table = cumulative_ranks(number_of, lean)
    lot = jax.random.randint(jax.random.fold_in(own_key, 1), extent, 0, int(table[number_of - 1]))
    standing = jnp.searchsorted(jnp.asarray(table, jnp.int32), lot, side="right")
    return jax.random.permutation(jax.random.fold_in(own_key, 2), number_of)[standing].astype(jnp.int32)


def gaussian(key, extent, deviation, most, shards=(), kind=jnp.bfloat16):
    drawn = jax.random.normal(key, extent, jnp.float32) * deviation
    if len(shards) > 0:
        drawn = block_levels(key, extent, shards, -0.22, 0.18) * drawn
    return jnp.clip(drawn, min=-most, max=most).astype(kind)


def setup_inputs(seed: int = 0) -> dict:
    seeds = jax.random.split(jax.random.key(seed), 6)
    own_rows = gaussian(seeds[0], (FRONTS, ROWS, W), 1.0, 6.0, ((0, 16), (1, 32)), jnp.float32)
    child_tile = draw_child_tile(jax.random.fold_in(seeds[5], 71), 0)
    col_map = jax.vmap(lambda own: jax.random.permutation(own, W))(jax.random.split(seeds[2], FRONTS)).reshape((FRONTS, W)).astype(jnp.int32)
    parent = plant(ranked_ids(seeds[3], (FRONTS,), FRONTS, 2), jax.random.fold_in(seeds[3], 3), 0, FRONTS - 1).astype(jnp.int32)
    live_rows = plant(jax.random.randint(seeds[4], (FRONTS,), ROWS // 8, ROWS + 1), jax.random.fold_in(seeds[4], 1), ROWS // 8, ROWS).astype(jnp.int32)
    return {"own_rows": own_rows, "child_tile": child_tile, "col_map": col_map, "parent": parent, "live_rows": live_rows}


def reference(own_rows, child_tile, col_map, parent, live_rows):
    highest = lax.Precision.HIGHEST

    def child_gram(pair):
        tile, cmap = pair
        mapped = jnp.zeros_like(tile).at[:, cmap].set(tile)
        return jnp.dot(mapped.T, mapped, precision=highest)
    grams = lax.map(child_gram, (child_tile, col_map))

    def one_front(items):
        own, live, index = items
        rowid = jnp.arange(ROWS, dtype=jnp.int32)
        own_live = jnp.where((rowid < live)[:, None], own, jnp.float32(0.0))
        owner = (parent == index).astype(jnp.float32)
        raw = jnp.dot(own_live.T, own_live, precision=highest)
        raw = raw + jnp.einsum('c,cij->ij', owner, grams, precision=highest)
        scale = (jnp.diagonal(raw) / ROWS + 1e-06) ** (-0.5)
        gram = scale[:, None] * raw * scale[None, :] + 0.25 * ROWS * jnp.eye(W, dtype=jnp.float32)
        lower = jnp.linalg.cholesky(gram)
        panel = lax.linalg.triangular_solve(lower, own_live * scale[None, :], left_side=False, lower=True, transpose_a=True)
        return (lower.T, panel)
    fronts = jnp.arange(FRONTS, dtype=jnp.int32)
    r_factor, q_panel = lax.map(one_front, (own_rows, live_rows, fronts))
    return (r_factor, q_panel)
```

```python
import jax
import jax.numpy as jnp
from jax import lax
from jax.experimental import pallas as pl
from jax.experimental.pallas import tpu as pltpu
from jax.sharding import PartitionSpec as P

F32 = jnp.float32
LB = 128
NN = ((1,), (0,))
TN = ((0,), (0,))
NT = ((1,), (1,))
VMEM = pl.BlockSpec(memory_space=pltpu.VMEM)
SMEM = pl.BlockSpec(memory_space=pltpu.SMEM)
PARAMS = pltpu.CompilerParams(vmem_limit_bytes=48 << 20)


def split(x):
    hi = x.astype(jnp.bfloat16)
    lo = (x - hi.astype(F32)).astype(jnp.bfloat16)
    return hi, lo


def dot(a, b, dims):
    return lax.dot_general(a, b, (dims, ((), ())), preferred_element_type=F32)


def dot3(a, b, dims):
    return dot(a[0], b[0], dims) + (dot(a[0], b[1], dims) + dot(a[1], b[0], dims))


def upper_blocks(width):
    n = width // LB
    return [(i, j) for i in range(n) for j in range(i, n)]


def map_kernel(tile_ref, map_ref, out_ref):
    width = tile_ref.shape[1]
    rows = tile_ref.shape[0]
    tile = tile_ref[...]
    first = tile.astype(jnp.bfloat16)
    rest = tile - first.astype(F32)
    second = rest.astype(jnp.bfloat16)
    third = (rest - second.astype(F32)).astype(jnp.bfloat16)
    parts = jnp.concatenate([first, second, third], axis=0)
    for i in range(width // LB):
        target = lax.broadcasted_iota(jnp.int32, (LB, width), 0) + i * LB
        onehot = (target == map_ref[...]).astype(F32).astype(jnp.bfloat16)
        moved = dot(parts, onehot, NT)
        out_ref[:, i * LB : (i + 1) * LB] = (
            moved[:rows] + moved[rows : 2 * rows] + moved[2 * rows :]
        )


def map_columns(tile, cmap):
    return pl.pallas_call(
        map_kernel,
        out_shape=jax.ShapeDtypeStruct(tile.shape, F32),
        in_specs=[VMEM, VMEM],
        out_specs=VMEM,
        compiler_params=PARAMS,
        name="map_columns",
    )(tile, cmap)


def gram_kernel(live_ref, own_ref, arrived_ref, out_ref, hi_ref, lo_ref):
    local, width = own_ref.shape
    rows = lax.broadcasted_iota(jnp.int32, own_ref.shape, 0)
    own = jnp.where(rows < live_ref[0], own_ref[...], F32(0))
    hi, lo = split(own)
    hi_ref[:local, :] = hi
    lo_ref[:local, :] = lo
    hi, lo = split(arrived_ref[...])
    hi_ref[local:, :] = hi
    lo_ref[local:, :] = lo
    at = 0
    for i in range(width // LB):
        left = slice(i * LB, (i + 1) * LB)
        right = slice(i * LB, width)
        strip = dot3(
            (hi_ref[:, left], lo_ref[:, left]), (hi_ref[:, right], lo_ref[:, right]), TN
        )
        for j in range(strip.shape[1] // LB):
            out_ref[at : at + LB, :] = strip[:, j * LB : (j + 1) * LB]
            at += LB


def packed_gram(live, own, arrived):
    total = own.shape[0] + arrived.shape[0]
    width = own.shape[1]
    return pl.pallas_call(
        gram_kernel,
        out_shape=jax.ShapeDtypeStruct((len(upper_blocks(width)) * LB, LB), F32),
        in_specs=[SMEM, VMEM, VMEM],
        out_specs=VMEM,
        scratch_shapes=[
            pltpu.VMEM((total, width), jnp.bfloat16),
            pltpu.VMEM((total, width), jnp.bfloat16),
        ],
        compiler_params=PARAMS,
        name="packed_gram",
    )(live, own, arrived)


def row8(x, i):
    return jnp.broadcast_to(x[i : i + 1, :], (8, LB))


def lane8(x, j):
    return jnp.broadcast_to(x[:, j : j + 1], (8, LB))


def total8(terms):
    while len(terms) > 1:
        terms = [terms[i] + terms[i + 1] for i in range(0, len(terms), 2)]
    return terms[0]


def factor_block(slabs):
    count = len(slabs)
    sub = lax.broadcasted_iota(jnp.int32, (8, LB), 0)
    lane = lax.broadcasted_iota(jnp.int32, (8, LB), 1)
    inv = [jnp.where(lane == sub + 8 * v, F32(1), F32(0)) for v in range(count)]
    slabs = list(slabs)
    r_out, inv_out = [], []
    for b in range(count):
        t, x = slabs[b], inv[b]
        cols = [lane8(t, 8 * b + j) for j in range(8)]
        a = [[row8(cols[j], i) if i <= j else None for j in range(8)] for i in range(8)]
        r = [row8(t, i) for i in range(8)]
        y = [row8(x, i) for i in range(8)]
        rd = [None] * 8
        m = [[None] * 8 for _ in range(8)]
        for k in range(8):
            rd[k] = 1.0 / a[k][k]
            for j in range(k + 1, 8):
                m[k][j] = a[k][j] * rd[k]
                for i in range(j, 8):
                    a[j][i] = a[j][i] - m[k][j] * a[k][i]
                r[j] = r[j] - m[k][j] * r[k]
                y[j] = y[j] - m[k][j] * y[k]
        pivots, rows, invs = a[0][0], r[0], y[0]
        for k in range(1, 8):
            pivots = jnp.where(sub == k, a[k][k], pivots)
            rows = jnp.where(sub == k, r[k], rows)
            invs = jnp.where(sub == k, y[k], invs)
        rs = lax.rsqrt(pivots)
        r_out.append(jnp.where(lane >= sub + 8 * b, rows * rs, F32(0)))
        inv_out.append(invs * rs)
        if b + 1 < count:
            z, w = [None] * 8, [None] * 8
            for k in reversed(range(8)):
                z[k] = r[k] * rd[k]
                w[k] = y[k] * rd[k]
                for i in range(k + 1, 8):
                    z[k] = z[k] - m[k][i] * z[i]
                    w[k] = w[k] - m[k][i] * w[i]
            for v in range(b + 1, count):
                cv = [lane8(slabs[v], 8 * b + j) for j in range(8)]
                slabs[v] = slabs[v] - total8([cv[j] * z[j] for j in range(8)])
                inv[v] = inv[v] - total8([cv[j] * w[j] for j in range(8)])
    return r_out, inv_out


def factor_kernel(total_rows, where_ref, packed_ref, own_ref, r_ref, q_ref, a_ref, inv_ref):
    local, width = own_ref.shape
    n = width // LB
    diag = lax.broadcasted_iota(jnp.int32, (LB, LB), 0) == lax.broadcasted_iota(
        jnp.int32, (LB, LB), 1
    )
    blocks = upper_blocks(width)
    across, down = [], []
    for i in range(n):
        at = blocks.index((i, i)) * LB
        only = jnp.where(diag, packed_ref[at : at + LB, :], F32(0))
        across.append(
            lax.rsqrt(jnp.sum(only, axis=0, keepdims=True) / total_rows + F32(1e-6))
        )
        down.append(lax.rsqrt(jnp.sum(only, axis=1, keepdims=True) / total_rows + F32(1e-6)))
    shift = jnp.where(diag, F32(0.25 * total_rows), F32(0))
    for at, (i, j) in enumerate(blocks):
        block = packed_ref[at * LB : (at + 1) * LB, :] * down[i] * across[j]
        if i == j:
            block = block + shift
        a_ref[i * LB : (i + 1) * LB, j * LB : (j + 1) * LB] = block
    rows = lax.broadcasted_iota(jnp.int32, (local, LB), 0)
    for j in range(n):
        cols = slice(j * LB, (j + 1) * LB)
        q_ref[:, cols] = jnp.where(rows < where_ref[0], own_ref[:, cols] * across[j], F32(0))
    column = lax.broadcasted_iota(jnp.int32, (LB, width), 1)

    def step(k, carry):
        o = pl.multiple_of(k * LB, LB)
        r_rows, inv_rows = factor_block(
            [a_ref[pl.ds(o + 8 * v, 8), pl.ds(o, LB)] for v in range(LB // 8)]
        )
        for v in range(LB // 8):
            inv_ref[8 * v : 8 * v + 8, :] = inv_rows[v]
        inv = split(inv_ref[...])
        strip = dot3(inv, split(a_ref[pl.ds(o, LB), :]), NN)
        strip = jnp.where(column >= o + LB, strip, F32(0))
        a_ref[pl.ds(o, LB), :] = strip
        for v in range(LB // 8):
            a_ref[pl.ds(o + 8 * v, 8), pl.ds(o, LB)] = r_rows[v]
        strip = split(strip)
        q_now = dot3(split(q_ref[:, pl.ds(o, LB)]), inv, NT)
        q_ref[...] = q_ref[...] - dot3(split(q_now), strip, NN)
        q_ref[:, pl.ds(o, LB)] = q_now

        def update(i, carry):
            oi = pl.multiple_of(i * LB, LB)
            mine = split(a_ref[pl.ds(o, LB), pl.ds(oi, LB)])
            a_ref[pl.ds(oi, LB), :] = a_ref[pl.ds(oi, LB), :] - dot3(mine, strip, TN)
            return carry

        lax.fori_loop(k + 1, n, update, 0)
        return carry

    lax.fori_loop(0, n, step, 0)
    r_ref[...] = a_ref[pl.ds(pl.multiple_of(where_ref[1], 8), r_ref.shape[0]), :]


def factor(where, packed, own, out_rows, total_rows):
    width = own.shape[1]
    return pl.pallas_call(
        lambda *refs: factor_kernel(total_rows, *refs),
        out_shape=(
            jax.ShapeDtypeStruct((out_rows, width), F32),
            jax.ShapeDtypeStruct(own.shape, F32),
        ),
        in_specs=[SMEM, VMEM, VMEM],
        out_specs=(VMEM, VMEM),
        scratch_shapes=[pltpu.VMEM((width, width), F32), pltpu.VMEM((LB, LB), F32)],
        compiler_params=PARAMS,
        name="factor",
    )(where, packed, own)


def shift_z(x, k, devices):
    return lax.ppermute(x, "rows", [(i, (i + 2 * k) % devices) for i in range(devices)])


def sum_over_rows(packed, devices):
    me = lax.axis_index("rows")
    core, z = me % 2, me // 2
    length = packed.shape[0]
    half, quarter = length // 2, length // 8
    pairs = [(i, i ^ 1) for i in range(devices)]
    chips = devices // 2
    classes = [
        [2 * (a + 4 * i) + c for i in range(chips // 4)] for c in range(2) for a in range(4)
    ]
    cut = lambda x, at, size: lax.dynamic_slice_in_dim(x, at, size, 0)
    mine = cut(packed, core * half, half) + lax.ppermute(
        cut(packed, (1 - core) * half, half), "rows", pairs
    )
    part = lambda k: cut(mine, ((z + k) % 4) * quarter, quarter)
    from_left = shift_z(part(1), 1, devices)
    from_right = shift_z(part(3), -1, devices)
    far = part(2)
    far_left = shift_z(far[: quarter // 2], 2, devices)
    far_right = shift_z(far[quarter // 2 :], -2, devices)
    summed = part(0) + from_left + from_right + jnp.concatenate([far_left, far_right])
    pieces = lax.all_to_all(
        summed, "rows", split_axis=0, concat_axis=0, axis_index_groups=classes, tiled=True
    )
    done = jnp.sum(pieces.reshape(chips // 4, -1, LB), axis=0)
    whole = lax.all_gather(done, "rows", axis=0, axis_index_groups=classes, tiled=True)
    left = shift_z(whole, 1, devices)
    right = shift_z(whole, -1, devices)
    far_left = shift_z(whole[: quarter // 2], 2, devices)
    far_right = shift_z(whole[quarter // 2 :], -2, devices)
    stack = jnp.stack([whole, right, jnp.concatenate([far_left, far_right]), left])
    order = (jnp.arange(4) - z) % 4
    mine = jnp.take(stack, order, axis=0).reshape(half, LB)
    other = lax.ppermute(mine, "rows", pairs)
    return jnp.where(
        core == 0, jnp.concatenate([mine, other]), jnp.concatenate([other, mine])
    )


def body(own_rows, child_tile, col_map, parent, live_rows):
    group = lax.axis_index("front")
    place = lax.axis_index("rows")
    groups = lax.axis_size("front")
    devices = lax.axis_size("rows")
    own, tile = own_rows[0], child_tile[0]
    local, width = own.shape
    tile_rows = tile.shape[0]
    fronts = jnp.arange(groups, dtype=jnp.int32)
    live = lax.dynamic_index_in_dim(live_rows, group, keepdims=False)
    my_parent = lax.dynamic_index_in_dim(parent, group, keepdims=False)
    mapped = map_columns(tile, lax.dynamic_slice_in_dim(col_map, group, 1, 0))
    buffer = jnp.where((fronts == my_parent)[:, None, None], mapped[None], F32(0))
    arrived = lax.all_to_all(buffer, "front", split_axis=0, concat_axis=0, tiled=True)
    where = jnp.stack([live - place * local, place * tile_rows]).astype(jnp.int32)
    packed = packed_gram(where, own, arrived.reshape(-1, width))
    packed = sum_over_rows(packed, devices)
    r_rows, panel = factor(where, packed, own, tile_rows, local * devices)
    return (r_rows[None], panel[None])


def solution(mesh):
    placed = (P("front", "rows", None), P("front", "rows", None), P(), P(), P())
    return jax.shard_map(
        body,
        mesh=mesh,
        in_specs=placed,
        out_specs=(P("front", "rows", None), P("front", "rows", None)),
        check_vma=False,
    )
```

```python
import functools

import jax
import jax.numpy as jnp
from jax import lax
from jax.experimental import pallas as pl
from jax.experimental.pallas import tpu as pltpu
from jax.sharding import PartitionSpec as P

F32 = jnp.float32
LB = 128
NN = ((1,), (0,))
TN = ((0,), (0,))
NT = ((1,), (1,))
VMEM = pl.BlockSpec(memory_space=pltpu.VMEM)
SMEM = pl.BlockSpec(memory_space=pltpu.SMEM)
PARAMS = pltpu.CompilerParams(vmem_limit_bytes=48 << 20)


def split(x):
    hi = x.astype(jnp.bfloat16)
    lo = (x - hi.astype(F32)).astype(jnp.bfloat16)
    return hi, lo


def dot(a, b, dims):
    return lax.dot_general(a, b, (dims, ((), ())), preferred_element_type=F32)


def dot3(a, b, dims):
    return dot(a[0], b[0], dims) + (dot(a[0], b[1], dims) + dot(a[1], b[0], dims))


def upper_blocks(width):
    n = width // LB
    return [(i, j) for i in range(n) for j in range(i, n)]


def place_kernel(at_ref, tile_ref, map_ref, out_ref):
    rows, width = tile_ref.shape
    tile = tile_ref[...]
    first = tile.astype(jnp.bfloat16)
    rest = tile - first.astype(F32)
    second = rest.astype(jnp.bfloat16)
    third = (rest - second.astype(F32)).astype(jnp.bfloat16)
    parts = jnp.concatenate([first, second, third], axis=0)
    columns = map_ref[pl.ds(at_ref[0], 1), :]
    out_ref[...] = jnp.zeros(out_ref.shape, F32)
    for i in range(width // LB):
        target = lax.broadcasted_iota(jnp.int32, (LB, width), 0) + i * LB
        onehot = (target == columns).astype(F32).astype(jnp.bfloat16)
        moved = dot(parts, onehot, NT)
        out_ref[at_ref[1], :, i * LB : (i + 1) * LB] = (
            moved[:rows] + moved[rows : 2 * rows] + moved[2 * rows :]
        )


def place_child(at, tile, col_map):
    return pl.pallas_call(
        place_kernel,
        out_shape=jax.ShapeDtypeStruct((col_map.shape[0],) + tile.shape, F32),
        in_specs=[SMEM, VMEM, VMEM],
        out_specs=VMEM,
        compiler_params=PARAMS,
        name="place_child",
    )(at, tile, col_map)


def own_gram_kernel(place_ref, own_ref, out_ref, hi_ref, lo_ref):
    width = own_ref.shape[1]
    rows = lax.broadcasted_iota(jnp.int32, own_ref.shape, 0)
    own = jnp.where(rows < place_ref[0], own_ref[...], F32(0))
    hi_ref[...], lo_ref[...] = split(own)
    at = 0
    for i in range(width // LB):
        left = slice(i * LB, (i + 1) * LB)
        right = slice(i * LB, width)
        strip = dot3(
            (hi_ref[:, left], lo_ref[:, left]), (hi_ref[:, right], lo_ref[:, right]), TN
        )
        for j in range(strip.shape[1] // LB):
            out_ref[at : at + LB, :] = strip[:, j * LB : (j + 1) * LB]
            at += LB


def own_gram(place, own):
    width = own.shape[1]
    return pl.pallas_call(
        own_gram_kernel,
        out_shape=jax.ShapeDtypeStruct((len(upper_blocks(width)) * LB, LB), F32),
        in_specs=[SMEM, VMEM],
        out_specs=VMEM,
        scratch_shapes=[pltpu.VMEM(own.shape, jnp.bfloat16)] * 2,
        compiler_params=PARAMS,
        name="own_gram",
    )(place, own)


def packed_rows(at, chip, half):
    quarter = half // 4
    piece = LB // 2
    side, first = divmod(at * LB, half)
    found = []
    for s in range(2):
        q, inner = divmod(first + s * piece, quarter)
        found.append(pl.multiple_of(((q + 4 - chip % 4) % 4) * quarter + inner, piece))
    return side, found


def gram_kernel(place_ref, mine_ref, arrived_ref, keep_ref, send_ref, hi_ref, lo_ref):
    width = arrived_ref.shape[1]
    half = keep_ref.shape[0]
    core, chip = place_ref[2], place_ref[3]
    hi_ref[...], lo_ref[...] = split(arrived_ref[...])
    piece = LB // 2
    at = 0
    for i in range(width // LB):
        left = slice(i * LB, (i + 1) * LB)
        right = slice(i * LB, width)
        strip = dot3(
            (hi_ref[:, left], lo_ref[:, left]), (hi_ref[:, right], lo_ref[:, right]), TN
        )
        for j in range(strip.shape[1] // LB):
            block = strip[:, j * LB : (j + 1) * LB] + mine_ref[at * LB : (at + 1) * LB, :]
            side, rows = packed_rows(at, chip, half)
            for s in range(2):

                def put(ref, s=s, rows=rows, block=block):
                    ref[pl.ds(rows[s], piece), :] = block[s * piece : (s + 1) * piece]

                pl.when(core == side)(lambda: put(keep_ref))
                pl.when(core != side)(lambda: put(send_ref))
            at += 1


def add_children(place, mine, arrived):
    half = jax.ShapeDtypeStruct((mine.shape[0] // 2, LB), F32)
    return pl.pallas_call(
        gram_kernel,
        out_shape=(half, half),
        in_specs=[SMEM, VMEM, VMEM],
        out_specs=(VMEM, VMEM),
        scratch_shapes=[pltpu.VMEM(arrived.shape, jnp.bfloat16)] * 2,
        compiler_params=PARAMS,
        name="add_children",
    )(place, mine, arrived)


def row8(x, i):
    return jnp.broadcast_to(x[i : i + 1, :], (8, LB))


def lane8(x, j):
    return jnp.broadcast_to(x[:, j : j + 1], (8, LB))


def total8(terms):
    while len(terms) > 1:
        terms = [terms[i] + terms[i + 1] for i in range(0, len(terms), 2)]
    return terms[0]


def factor_block(slabs):
    count, panel = len(slabs), 4
    sub = lax.broadcasted_iota(jnp.int32, (8, LB), 0)
    lane = lax.broadcasted_iota(jnp.int32, (8, LB), 1)
    inv = [jnp.where(lane == sub + 8 * v, F32(1), F32(0)) for v in range(count)]
    slabs = list(slabs)
    r_out, inv_out = [], []
    for p in range(0, count, panel):
        end = p + panel
        here = [jnp.maximum(lane8(slabs[p], 8 * p + j), F32(-3e38)) for j in range(8)]
        for b in range(p, end):
            a = [[row8(here[j], i) if i <= j else None for j in range(8)] for i in range(8)]
            r = [row8(slabs[b], i) for i in range(8)]
            y = [row8(inv[b], i) for i in range(8)]
            rd = [None] * 8
            m = [[None] * 8 for _ in range(8)]
            vectors = [r, y]
            if b + 1 < end:
                c = [lane8(slabs[b + 1], 8 * b + j) for j in range(8)]
                here = [lane8(slabs[b + 1], 8 * (b + 1) + j) for j in range(8)]
                vectors.append(c)
            for k in range(8):
                rd[k] = 1.0 / a[k][k]
                for j in range(k + 1, 8):
                    m[k][j] = a[k][j] * rd[k]
                    for i in range(j, 8):
                        a[j][i] = a[j][i] - m[k][j] * a[k][i]
                    for vector in vectors:
                        vector[j] = vector[j] - m[k][j] * vector[k]
            pivots, rows, invs = a[0][0], r[0], y[0]
            for k in range(1, 8):
                pivots = jnp.where(sub == k, a[k][k], pivots)
                rows = jnp.where(sub == k, r[k], rows)
                invs = jnp.where(sub == k, y[k], invs)
            rs = lax.rsqrt(pivots)
            r_out.append(jnp.where(lane >= sub + 8 * b, rows * rs, F32(0)))
            inv_out.append(invs * rs)
            if b + 1 == end:
                continue
            u = [c[j] * rd[j] for j in range(8)]
            for j in range(8):
                slabs[b + 1] = slabs[b + 1] - u[j] * r[j]
                inv[b + 1] = inv[b + 1] - u[j] * y[j]
            for j in range(8):
                for k in range(8):
                    here[j] = here[j] - u[k] * row8(c[k], j)
            if b + 2 == end:
                continue
            z, w = [None] * 8, [None] * 8
            for k in reversed(range(8)):
                z[k] = r[k] * rd[k]
                w[k] = y[k] * rd[k]
                for i in range(k + 1, 8):
                    z[k] = z[k] - m[k][i] * z[i]
                    w[k] = w[k] - m[k][i] * w[i]
            for v in range(b + 2, end):
                cv = [lane8(slabs[v], 8 * b + j) for j in range(8)]
                slabs[v] = slabs[v] - total8([cv[j] * z[j] for j in range(8)])
                inv[v] = inv[v] - total8([cv[j] * w[j] for j in range(8)])
        if end < count:
            both = jnp.concatenate(
                [jnp.concatenate(x[p:end], axis=0) for x in (r_out, inv_out)], axis=1
            )
            hi, lo = split(both)
            taken = dot(
                jnp.concatenate([hi[:, :LB], hi[:, :LB], lo[:, :LB]], axis=0),
                jnp.concatenate([hi, lo, hi], axis=0),
                TN,
            )
            for v in range(end, count):
                slabs[v] = slabs[v] - taken[8 * v : 8 * v + 8, :LB]
                inv[v] = inv[v] - taken[8 * v : 8 * v + 8, LB:]
    return r_out, inv_out


def tall(a, axis):
    return jnp.concatenate([a[0], a[0], a[1]], axis=axis)


def wide(b, axis):
    return jnp.concatenate([b[0], b[1], b[0]], axis=axis)


def product(a, b, dims):
    return dot(tall(a, dims[0][0]), wide(b, dims[1][0]), dims)


def factor_kernel(
    total_rows, place_ref, mine_ref, other_ref, own_ref, r_ref, q_ref,
    a_ref, inv_ref, strip_ref, q_now_ref,
):
    local, width = own_ref.shape
    n = width // LB
    half = mine_ref.shape[0]
    core, chip = place_ref[2], place_ref[3]
    diag = lax.broadcasted_iota(jnp.int32, (LB, LB), 0) == lax.broadcasted_iota(
        jnp.int32, (LB, LB), 1
    )
    blocks = upper_blocks(width)

    def fetch(at):
        side, rows = packed_rows(at, chip, half)
        parts = [
            jnp.where(
                core == side, mine_ref[pl.ds(o, LB // 2), :], other_ref[pl.ds(o, LB // 2), :]
            )
            for o in rows
        ]
        return jnp.concatenate(parts, axis=0)

    across, down = [], []
    for i in range(n):
        only = jnp.where(diag, fetch(blocks.index((i, i))), F32(0))
        across.append(
            lax.rsqrt(jnp.sum(only, axis=0, keepdims=True) / total_rows + F32(1e-6))
        )
        down.append(lax.rsqrt(jnp.sum(only, axis=1, keepdims=True) / total_rows + F32(1e-6)))
    shift = jnp.where(diag, F32(0.25 * total_rows), F32(0))
    for at, (i, j) in enumerate(blocks):
        block = fetch(at) * down[i] * across[j]
        if i == j:
            block = block + shift
        a_ref[i * LB : (i + 1) * LB, j * LB : (j + 1) * LB] = block
    rows = lax.broadcasted_iota(jnp.int32, (local, LB), 0)
    for j in range(n):
        cols = slice(j * LB, (j + 1) * LB)
        q_ref[:, cols] = jnp.where(rows < place_ref[0], own_ref[:, cols] * across[j], F32(0))
    strip_ref[...] = jnp.zeros(strip_ref.shape, F32)
    q_now_ref[...] = jnp.zeros(q_now_ref.shape, F32)

    def step(first, k, carry):
        o = pl.multiple_of(k * LB, LB)
        left = first * LB
        slabs = [a_ref[pl.ds(o + 8 * v, 8), pl.ds(o, LB)] for v in range(LB // 8)]
        old = split(strip_ref[...])
        old_tall, old_wide = tall(old, 0), wide(old, 0)
        for i in range(first, n):
            at = slice(i * LB, (i + 1) * LB)
            a_ref[at, i * LB :] = a_ref[at, i * LB :] - dot(
                old_tall[:, at], old_wide[:, i * LB :], TN
            )
        q_ref[:, left:] = q_ref[:, left:] - dot(
            tall(split(q_now_ref[...]), 1), old_wide[:, left:], NN
        )
        r_rows, inv_rows = factor_block(slabs)
        for v in range(LB // 8):
            inv_ref[8 * v : 8 * v + 8, :] = inv_rows[v]
        inv = split(inv_ref[...])
        strip = product(inv, split(a_ref[pl.ds(o, LB), left:]), NN)
        column = lax.broadcasted_iota(jnp.int32, strip.shape, 1) + left
        strip = jnp.where(column >= o + LB, strip, F32(0))
        strip_ref[:, left:] = strip
        a_ref[pl.ds(o, LB), left:] = strip
        for v in range(LB // 8):
            a_ref[pl.ds(o + 8 * v, 8), pl.ds(o, LB)] = r_rows[v]
        after = pl.multiple_of(jnp.minimum(k + 1, n - 1) * LB, LB)
        new = split(strip_ref[:, pl.ds(after, LB)])
        a_ref[pl.ds(after, LB), pl.ds(after, LB)] = a_ref[
            pl.ds(after, LB), pl.ds(after, LB)
        ] - product(new, new, TN)
        q_now = product(split(q_ref[:, pl.ds(o, LB)]), inv, NT)
        q_now_ref[...] = q_now
        q_ref[:, pl.ds(o, LB)] = q_now
        return carry

    for first in (0, n // 2):
        lax.fori_loop(first, first + n // 2, functools.partial(step, first), 0)
    start = pl.multiple_of(place_ref[1], 8)
    mine = a_ref[pl.ds(start, r_ref.shape[0]), :]
    row = start + lax.broadcasted_iota(jnp.int32, mine.shape, 0)
    column = lax.broadcasted_iota(jnp.int32, mine.shape, 1)
    r_ref[...] = jnp.where(column >= row, mine, F32(0))


def factor(place, mine, other, own, out_rows, total_rows):
    local, width = own.shape
    return pl.pallas_call(
        functools.partial(factor_kernel, total_rows),
        out_shape=(
            jax.ShapeDtypeStruct((out_rows, width), F32),
            jax.ShapeDtypeStruct(own.shape, F32),
        ),
        in_specs=[SMEM, VMEM, VMEM, VMEM],
        out_specs=(VMEM, VMEM),
        scratch_shapes=[
            pltpu.VMEM((width, width), F32),
            pltpu.VMEM((LB, LB), F32),
            pltpu.VMEM((LB, width), F32),
            pltpu.VMEM((local, LB), F32),
        ],
        compiler_params=PARAMS,
        name="factor",
    )(place, mine, other, own)


def to_chip(x, k):
    devices = lax.axis_size("rows")
    return lax.ppermute(x, "rows", [(i, (i + 2 * k) % devices) for i in range(devices)])


def to_core(x):
    return lax.ppermute(x, "rows", [(i, i ^ 1) for i in range(lax.axis_size("rows"))])


def sum_over_rows(keep, send):
    chips = lax.axis_size("rows") // 2
    classes = [
        [2 * (a + 4 * i) + c for i in range(chips // 4)] for c in range(2) for a in range(4)
    ]
    quarter = keep.shape[0] // 4
    got = to_core(send)
    part = [
        keep[k * quarter : (k + 1) * quarter] + got[k * quarter : (k + 1) * quarter]
        for k in range(4)
    ]
    passing = to_chip(part[2], -1)
    before = to_chip(part[1], 1)
    after = to_chip(passing + part[3], -1)
    summed = part[0] + before + after
    pieces = lax.all_to_all(
        summed, "rows", split_axis=0, concat_axis=0, axis_index_groups=classes, tiled=True
    )
    done = jnp.sum(pieces.reshape(chips // 4, -1, LB), axis=0)
    whole = lax.all_gather(done, "rows", axis=0, axis_index_groups=classes, tiled=True)
    right = to_chip(whole, -1)
    left = to_chip(whole, 1)
    far = to_chip(right, -1)
    mine = jnp.concatenate([whole, right, far, left])
    return mine, to_core(mine)


def body(own_rows, child_tile, col_map, parent, live_rows):
    group = lax.axis_index("front")
    place = lax.axis_index("rows")
    own, tile = own_rows[0], child_tile[0]
    local, width = own.shape
    tile_rows = tile.shape[0]
    live = lax.dynamic_index_in_dim(live_rows, group, keepdims=False)
    my_parent = lax.dynamic_index_in_dim(parent, group, keepdims=False)
    at = jnp.stack([group, my_parent]).astype(jnp.int32)
    arrived = lax.all_to_all(
        place_child(at, tile, col_map), "front", split_axis=0, concat_axis=0, tiled=True
    )
    where = jnp.stack(
        [live - place * local, place * tile_rows, place % 2, place // 2]
    ).astype(jnp.int32)
    keep, send = add_children(where, own_gram(where, own), arrived.reshape(-1, width))
    mine, other = sum_over_rows(keep, send)
    r_rows, panel = factor(
        where, mine, other, own, tile_rows, local * lax.axis_size("rows")
    )
    return (r_rows[None], panel[None])


def solution(mesh):
    placed = (P("front", "rows", None), P("front", "rows", None), P(), P(), P())
    return jax.shard_map(
        body,
        mesh=mesh,
        in_specs=placed,
        out_specs=(P("front", "rows", None), P("front", "rows", None)),
        check_vma=False,
    )
```

```python
import functools

import jax
import jax.numpy as jnp
from jax import lax
from jax.experimental import pallas as pl
from jax.experimental.pallas import tpu as pltpu
from jax.sharding import PartitionSpec as P

F32 = jnp.float32
LB = 128
NN = ((1,), (0,))
TN = ((0,), (0,))
NT = ((1,), (1,))
VMEM = pl.BlockSpec(memory_space=pltpu.VMEM)
SMEM = pl.BlockSpec(memory_space=pltpu.SMEM)
PARAMS = pltpu.CompilerParams(vmem_limit_bytes=32 << 20)


def split(x):
    hi = x.astype(jnp.bfloat16)
    lo = (x - hi.astype(F32)).astype(jnp.bfloat16)
    return hi, lo


def dot(a, b, dims):
    return lax.dot_general(a, b, (dims, ((), ())), preferred_element_type=F32)


def dot3(a, b, dims):
    return dot(a[0], b[0], dims) + (dot(a[0], b[1], dims) + dot(a[1], b[0], dims))


def upper_blocks(width):
    n = width // LB
    return [(i, j) for i in range(n) for j in range(i, n)]


def place_kernel(parent_ref, tile_ref, map_ref, out_ref, moved_ref, sem):
    rows, width = tile_ref.shape
    group = lax.axis_index("front")
    tile = tile_ref[...]
    first = tile.astype(jnp.bfloat16)
    rest = tile - first.astype(F32)
    second = rest.astype(jnp.bfloat16)
    third = (rest - second.astype(F32)).astype(jnp.bfloat16)
    parts = jnp.concatenate([first, second, third], axis=0)
    columns = map_ref[pl.ds(group, 1), :]
    for i in range(width // LB):
        target = lax.broadcasted_iota(jnp.int32, (LB, width), 0) + i * LB
        onehot = (target == columns).astype(F32).astype(jnp.bfloat16)
        moved = dot(parts, onehot, NT)
        moved_ref[:, i * LB : (i + 1) * LB] = (
            moved[:rows] + moved[rows : 2 * rows] + moved[2 * rows :]
        )
    copy = pltpu.make_async_copy(moved_ref, out_ref.at[parent_ref[group]], sem)
    copy.start()
    copy.wait()


def place_child(parent, tile, col_map):
    return pl.pallas_call(
        place_kernel,
        out_shape=jax.ShapeDtypeStruct((col_map.shape[0],) + tile.shape, F32),
        in_specs=[SMEM, VMEM, VMEM],
        out_specs=pl.BlockSpec(memory_space=pl.ANY),
        scratch_shapes=[pltpu.VMEM(tile.shape, F32), pltpu.SemaphoreType.DMA(())],
        compiler_params=PARAMS,
        name="place_child",
    )(parent, tile, col_map)


def live_here(live_ref, local):
    return live_ref[lax.axis_index("front")] - lax.axis_index("rows") * local


def own_gram_kernel(live_ref, own_ref, out_ref, hi_ref, lo_ref):
    local, width = own_ref.shape
    rows = lax.broadcasted_iota(jnp.int32, own_ref.shape, 0)
    own = jnp.where(rows < live_here(live_ref, local), own_ref[...], F32(0))
    hi_ref[...], lo_ref[...] = split(own)
    at = 0
    for i in range(width // LB):
        left = slice(i * LB, (i + 1) * LB)
        right = slice(i * LB, width)
        strip = dot3(
            (hi_ref[:, left], lo_ref[:, left]), (hi_ref[:, right], lo_ref[:, right]), TN
        )
        for j in range(strip.shape[1] // LB):
            out_ref[at : at + LB, :] = strip[:, j * LB : (j + 1) * LB]
            at += LB


def own_gram(live_rows, own):
    width = own.shape[1]
    return pl.pallas_call(
        own_gram_kernel,
        out_shape=jax.ShapeDtypeStruct((len(upper_blocks(width)) * LB, LB), F32),
        in_specs=[SMEM, VMEM],
        out_specs=VMEM,
        scratch_shapes=[pltpu.VMEM(own.shape, jnp.bfloat16)] * 2,
        compiler_params=PARAMS,
        name="own_gram",
    )(live_rows, own)


def packed_rows(at, chip, half):
    quarter = half // 4
    piece = LB // 2
    side, first = divmod(at * LB, half)
    turn = chip % 4
    found = []
    for s in range(2):
        q, inner = divmod(first + s * piece, quarter)
        position = (q + 4 - turn) % 4 if side == 0 else (turn + 4 - q) % 4
        found.append(pl.multiple_of(position * quarter + inner, piece))
    return side, found


CHUNK = 128


def gram_kernel(parent_ref, mine_ref, arrived_ref, keep_ref, send_ref, hi_ref, lo_ref, sum_ref):
    children, rows, width = arrived_ref.shape
    half = keep_ref.shape[0]
    group = lax.axis_index("front")
    core, chip = lax.axis_index("rows") % 2, lax.axis_index("rows") // 2

    def pack(child, count):
        mine = parent_ref[child] == group

        @pl.when(mine)
        def _():
            at = pl.ds(pl.multiple_of(count * rows, rows), rows)
            hi_ref[at, :], lo_ref[at, :] = split(arrived_ref[child])

        return count + mine.astype(jnp.int32)

    count = lax.fori_loop(0, children, pack, jnp.int32(0))
    each = CHUNK // rows
    chunks = (count + each - 1) // each
    empty = jnp.zeros((rows, width), jnp.bfloat16)

    def clear(child, carry):
        at = pl.ds(pl.multiple_of(child * rows, rows), rows)
        hi_ref[at, :] = empty
        lo_ref[at, :] = empty
        return carry

    lax.fori_loop(count, jnp.maximum(chunks, 1) * each, clear, 0)

    def add(chunk, base_ref):
        at_rows = pl.ds(pl.multiple_of(chunk * CHUNK, CHUNK), CHUNK)
        at = 0
        for i in range(width // LB):
            left = slice(i * LB, (i + 1) * LB)
            right = slice(i * LB, width)
            strip = dot3(
                (hi_ref[at_rows, left], lo_ref[at_rows, left]),
                (hi_ref[at_rows, right], lo_ref[at_rows, right]),
                TN,
            )
            for j in range(strip.shape[1] // LB):
                here = slice(at, at + LB)
                sum_ref[here, :] = strip[:, j * LB : (j + 1) * LB] + base_ref[here, :]
                at += LB

    add(0, mine_ref)

    def more(chunk, carry):
        add(chunk, sum_ref)
        return carry

    lax.fori_loop(1, chunks, more, 0)
    piece = LB // 2

    def hand_out(refs):
        for at in range(mine_ref.shape[0] // LB):
            side, first = packed_rows(at, chip, half)
            for s in range(2):
                refs[side][pl.ds(first[s], piece), :] = sum_ref[
                    at * LB + s * piece : at * LB + (s + 1) * piece, :
                ]

    pl.when(core == 0)(lambda: hand_out((keep_ref, send_ref)))
    pl.when(core == 1)(lambda: hand_out((send_ref, keep_ref)))


def add_children(parent, mine, arrived):
    children, rows, width = arrived.shape
    half = jax.ShapeDtypeStruct((mine.shape[0] // 2, LB), F32)
    return pl.pallas_call(
        gram_kernel,
        out_shape=(half, half),
        in_specs=[SMEM, VMEM, VMEM],
        out_specs=(VMEM, VMEM),
        scratch_shapes=[pltpu.VMEM((children * rows, width), jnp.bfloat16)] * 2
        + [pltpu.VMEM(mine.shape, F32)],
        compiler_params=PARAMS,
        name="add_children",
    )(parent, mine, arrived)


def row8(x, i):
    return jnp.broadcast_to(x[i : i + 1, :], (8, LB))


def lane8(x, j):
    return jnp.broadcast_to(x[:, j : j + 1], (8, LB))


def total8(terms):
    while len(terms) > 1:
        terms = [terms[i] + terms[i + 1] for i in range(0, len(terms), 2)]
    return terms[0]


def factor_block(slabs):
    count, panel, ahead = len(slabs), 4, 2
    sub = lax.broadcasted_iota(jnp.int32, (8, LB), 0)
    lane = lax.broadcasted_iota(jnp.int32, (8, LB), 1)
    inv = [jnp.where(lane == sub + 8 * v, F32(1), F32(0)) for v in range(count)]
    slabs = list(slabs)
    r_out, inv_out = [], []
    here = [jnp.maximum(lane8(slabs[0], j), F32(-3e38)) for j in range(8)]
    for p in range(0, count, panel):
        end = p + panel
        reach = min(end + ahead, count)
        for b in range(p, end):
            a = [[row8(here[j], i) if i <= j else None for j in range(8)] for i in range(8)]
            r = [row8(slabs[b], i) for i in range(8)]
            y = [row8(inv[b], i) for i in range(8)]
            rd = [None] * 8
            m = [[None] * 8 for _ in range(8)]
            vectors = [r, y]
            if b + 1 < reach:
                c = [lane8(slabs[b + 1], 8 * b + j) for j in range(8)]
                here = [lane8(slabs[b + 1], 8 * (b + 1) + j) for j in range(8)]
                vectors.append(c)
            for k in range(8):
                rd[k] = 1.0 / a[k][k]
                for j in range(k + 1, 8):
                    m[k][j] = a[k][j] * rd[k]
                    for i in range(j, 8):
                        a[j][i] = a[j][i] - m[k][j] * a[k][i]
                    for vector in vectors:
                        vector[j] = vector[j] - m[k][j] * vector[k]
            pivots, rows, invs = a[0][0], r[0], y[0]
            for k in range(1, 8):
                pivots = jnp.where(sub == k, a[k][k], pivots)
                rows = jnp.where(sub == k, r[k], rows)
                invs = jnp.where(sub == k, y[k], invs)
            rs = lax.rsqrt(pivots)
            r_out.append(jnp.where(lane >= sub + 8 * b, rows * rs, F32(0)))
            inv_out.append(invs * rs)
            if b + 1 == reach:
                continue
            u = [c[j] * rd[j] for j in range(8)]
            for j in range(8):
                slabs[b + 1] = slabs[b + 1] - u[j] * r[j]
                inv[b + 1] = inv[b + 1] - u[j] * y[j]
            for j in range(8):
                for k in range(8):
                    here[j] = here[j] - u[k] * row8(c[k], j)
            if b + 2 == reach:
                continue
            z, w = [None] * 8, [None] * 8
            for k in reversed(range(8)):
                z[k] = r[k] * rd[k]
                w[k] = y[k] * rd[k]
                for i in range(k + 1, 8):
                    z[k] = z[k] - m[k][i] * z[i]
                    w[k] = w[k] - m[k][i] * w[i]
            for v in range(b + 2, reach):
                cv = [lane8(slabs[v], 8 * b + j) for j in range(8)]
                slabs[v] = slabs[v] - total8([cv[j] * z[j] for j in range(8)])
                inv[v] = inv[v] - total8([cv[j] * w[j] for j in range(8)])
        if reach < count:
            both = jnp.concatenate(
                [jnp.concatenate(x[p:end], axis=0) for x in (r_out, inv_out)], axis=1
            )
            hi, lo = split(both)
            taken = dot(
                jnp.concatenate([hi[:, :LB], hi[:, :LB], lo[:, :LB]], axis=0),
                jnp.concatenate([hi, lo, hi], axis=0),
                TN,
            )
            for v in range(reach, count):
                slabs[v] = slabs[v] - taken[8 * v : 8 * v + 8, :LB]
                inv[v] = inv[v] - taken[8 * v : 8 * v + 8, LB:]
    return r_out, inv_out


def tall(a, axis):
    return jnp.concatenate([a[0], a[0], a[1]], axis=axis)


def wide(b, axis):
    return jnp.concatenate([b[0], b[1], b[0]], axis=axis)


def product(a, b, dims):
    return dot(tall(a, dims[0][0]), wide(b, dims[1][0]), dims)


def factor_kernel(
    total_rows, live_ref, mine_ref, other_ref, own_ref, r_ref, q_ref,
    a_ref, inv_ref, strip_ref, q_now_ref,
):
    local, width = own_ref.shape
    n = width // LB
    half = mine_ref.shape[0]
    place = lax.axis_index("rows")
    core, chip = place % 2, place // 2
    diag = lax.broadcasted_iota(jnp.int32, (LB, LB), 0) == lax.broadcasted_iota(
        jnp.int32, (LB, LB), 1
    )
    blocks = upper_blocks(width)

    def fetch(at):
        side, rows = packed_rows(at, chip, half)
        parts = [
            jnp.where(
                core == side, mine_ref[pl.ds(o, LB // 2), :], other_ref[pl.ds(o, LB // 2), :]
            )
            for o in rows
        ]
        return jnp.concatenate(parts, axis=0)

    across, down = [], []
    for i in range(n):
        only = jnp.where(diag, fetch(blocks.index((i, i))), F32(0))
        across.append(
            lax.rsqrt(jnp.sum(only, axis=0, keepdims=True) / total_rows + F32(1e-6))
        )
        down.append(lax.rsqrt(jnp.sum(only, axis=1, keepdims=True) / total_rows + F32(1e-6)))
    shift = jnp.where(diag, F32(0.25 * total_rows), F32(0))
    for at, (i, j) in enumerate(blocks):
        block = fetch(at) * down[i] * across[j]
        if i == j:
            block = block + shift
        a_ref[i * LB : (i + 1) * LB, j * LB : (j + 1) * LB] = block
    rows = lax.broadcasted_iota(jnp.int32, (local, LB), 0)
    live = live_here(live_ref, local)
    for j in range(n):
        cols = slice(j * LB, (j + 1) * LB)
        q_ref[:, cols] = jnp.where(rows < live, own_ref[:, cols] * across[j], F32(0))
    strip_ref[...] = jnp.zeros(strip_ref.shape, F32)
    q_now_ref[...] = jnp.zeros(q_now_ref.shape, F32)

    def step(first, k, carry):
        o = pl.multiple_of(k * LB, LB)
        left = first * LB
        slabs = [a_ref[pl.ds(o + 8 * v, 8), pl.ds(o, LB)] for v in range(LB // 8)]
        old = split(strip_ref[...])
        old_tall, old_wide = tall(old, 0), wide(old, 0)
        for i in range(first, n):
            at = slice(i * LB, (i + 1) * LB)
            a_ref[at, i * LB :] = a_ref[at, i * LB :] - dot(
                old_tall[:, at], old_wide[:, i * LB :], TN
            )
        q_ref[:, left:] = q_ref[:, left:] - dot(
            tall(split(q_now_ref[...]), 1), old_wide[:, left:], NN
        )
        r_rows, inv_rows = factor_block(slabs)
        for v in range(LB // 8):
            inv_ref[8 * v : 8 * v + 8, :] = inv_rows[v]
        inv = split(inv_ref[...])
        strip = product(inv, split(a_ref[pl.ds(o, LB), left:]), NN)
        column = lax.broadcasted_iota(jnp.int32, strip.shape, 1) + left
        strip = jnp.where(column >= o + LB, strip, F32(0))
        strip_ref[:, left:] = strip
        a_ref[pl.ds(o, LB), left:] = strip
        for v in range(LB // 8):
            a_ref[pl.ds(o + 8 * v, 8), pl.ds(o, LB)] = r_rows[v]
        after = pl.multiple_of(jnp.minimum(k + 1, n - 1) * LB, LB)
        new = split(strip_ref[:, pl.ds(after, LB)])
        a_ref[pl.ds(after, LB), pl.ds(after, LB)] = a_ref[
            pl.ds(after, LB), pl.ds(after, LB)
        ] - product(new, new, TN)
        q_now = product(split(q_ref[:, pl.ds(o, LB)]), inv, NT)
        q_now_ref[...] = q_now
        q_ref[:, pl.ds(o, LB)] = q_now
        return carry

    for first in (0, n // 2):
        lax.fori_loop(first, first + n // 2, functools.partial(step, first), 0)
    start = pl.multiple_of(place * r_ref.shape[0], r_ref.shape[0])
    mine = a_ref[pl.ds(start, r_ref.shape[0]), :]
    row = start + lax.broadcasted_iota(jnp.int32, mine.shape, 0)
    column = lax.broadcasted_iota(jnp.int32, mine.shape, 1)
    r_ref[...] = jnp.where(column >= row, mine, F32(0))


def factor(live_rows, mine, other, own, out_rows, total_rows):
    local, width = own.shape
    return pl.pallas_call(
        functools.partial(factor_kernel, total_rows),
        out_shape=(
            jax.ShapeDtypeStruct((out_rows, width), F32),
            jax.ShapeDtypeStruct(own.shape, F32),
        ),
        in_specs=[SMEM, VMEM, VMEM, VMEM],
        out_specs=(VMEM, VMEM),
        scratch_shapes=[
            pltpu.VMEM((width, width), F32),
            pltpu.VMEM((LB, LB), F32),
            pltpu.VMEM((LB, width), F32),
            pltpu.VMEM((local, LB), F32),
        ],
        compiler_params=PARAMS,
        name="factor",
    )(live_rows, mine, other, own)


def to_chip(x, k):
    devices = lax.axis_size("rows")
    pairs = [(i, (i + (2 * k if i % 2 == 0 else -2 * k)) % devices) for i in range(devices)]
    return lax.ppermute(x, "rows", pairs)


def to_core(x):
    return lax.ppermute(x, "rows", [(i, i ^ 1) for i in range(lax.axis_size("rows"))])


def sum_over_rows(keep, send):
    chips = lax.axis_size("rows") // 2
    classes = [
        [2 * (a + 4 * i) + c for i in range(chips // 4)] for c in range(2) for a in range(4)
    ]
    quarter = keep.shape[0] // 4
    got = to_core(send)
    part = [
        keep[k * quarter : (k + 1) * quarter] + got[k * quarter : (k + 1) * quarter]
        for k in range(4)
    ]
    passing = to_chip(part[2], -1)
    before = to_chip(part[1], 1)
    after = to_chip(passing + part[3], -1)
    summed = part[0] + before + after
    pieces = lax.all_to_all(
        summed, "rows", split_axis=0, concat_axis=0, axis_index_groups=classes, tiled=True
    )
    done = jnp.sum(pieces.reshape(chips // 4, -1, LB), axis=0)
    whole = lax.all_gather(done, "rows", axis=0, axis_index_groups=classes, tiled=True)
    right = to_chip(whole, -1)
    left = to_chip(whole, 1)
    far = to_chip(right, -1)
    mine = jnp.concatenate([whole, right, far, left])
    return mine, to_core(mine)


def body(own_rows, child_tile, col_map, parent, live_rows):
    own, tile = own_rows[0], child_tile[0]
    arrived = lax.all_to_all(
        place_child(parent, tile, col_map), "front", split_axis=0, concat_axis=0, tiled=True
    )
    keep, send = add_children(parent, own_gram(live_rows, own), arrived)
    mine, other = sum_over_rows(keep, send)
    total_rows = own.shape[0] * lax.axis_size("rows")
    r_rows, panel = factor(live_rows, mine, other, own, tile.shape[0], total_rows)
    return (r_rows[None], panel[None])


def solution(mesh):
    placed = (P("front", "rows", None), P("front", "rows", None), P(), P(), P())
    return jax.shard_map(
        body,
        mesh=mesh,
        in_specs=placed,
        out_specs=(P("front", "rows", None), P("front", "rows", None)),
        check_vma=False,
    )
```

```python
import functools

import jax
import jax.numpy as jnp
from jax import lax
from jax.experimental import pallas as pl
from jax.experimental.pallas import tpu as pltpu
from jax.sharding import PartitionSpec as P

F32 = jnp.float32
LB = 128
NN = ((1,), (0,))
TN = ((0,), (0,))
NT = ((1,), (1,))
VMEM = pl.BlockSpec(memory_space=pltpu.VMEM)
SMEM = pl.BlockSpec(memory_space=pltpu.SMEM)
ANY = pl.BlockSpec(memory_space=pl.ANY)
PARAMS = pltpu.CompilerParams(vmem_limit_bytes=32 << 20)


def split(x):
    hi = x.astype(jnp.bfloat16)
    lo = (x - hi.astype(F32)).astype(jnp.bfloat16)
    return hi, lo


def dot(a, b, dims):
    return lax.dot_general(a, b, (dims, ((), ())), preferred_element_type=F32)


def dot3(a, b, dims):
    return dot(a[0], b[0], dims) + (dot(a[0], b[1], dims) + dot(a[1], b[0], dims))


def upper_blocks(width):
    n = width // LB
    return [(i, j) for i in range(n) for j in range(i, n)]


def place_kernel(parent_ref, tile_hbm, map_hbm, out_ref, tile_ref, map_ref, moved_ref, sems):
    rows, width = tile_ref.shape
    group = lax.axis_index("front")
    fetches = [
        pltpu.make_async_copy(tile_hbm, tile_ref, sems.at[0]),
        pltpu.make_async_copy(map_hbm, map_ref, sems.at[1]),
    ]
    for fetch in fetches:
        fetch.start()
    for fetch in fetches:
        fetch.wait()
    tile = tile_ref[...]
    first = tile.astype(jnp.bfloat16)
    rest = tile - first.astype(F32)
    second = rest.astype(jnp.bfloat16)
    third = (rest - second.astype(F32)).astype(jnp.bfloat16)
    parts = jnp.concatenate([first, second, third], axis=0)
    columns = map_ref[pl.ds(group, 1), :]
    for i in range(width // LB):
        target = lax.broadcasted_iota(jnp.int32, (LB, width), 0) + i * LB
        onehot = (target == columns).astype(F32).astype(jnp.bfloat16)
        moved = dot(parts, onehot, NT)
        moved_ref[:, i * LB : (i + 1) * LB] = (
            moved[:rows] + moved[rows : 2 * rows] + moved[2 * rows :]
        )
    copy = pltpu.make_async_copy(moved_ref, out_ref.at[parent_ref[group]], sems.at[2])
    copy.start()
    copy.wait()


def place_child(parent, tile, col_map):
    return pl.pallas_call(
        place_kernel,
        out_shape=jax.ShapeDtypeStruct((col_map.shape[0],) + tile.shape, F32),
        in_specs=[SMEM, ANY, ANY],
        out_specs=ANY,
        scratch_shapes=[
            pltpu.VMEM(tile.shape, F32),
            pltpu.VMEM(col_map.shape, jnp.int32),
            pltpu.VMEM(tile.shape, F32),
            pltpu.SemaphoreType.DMA((3,)),
        ],
        compiler_params=PARAMS,
        name="place_child",
    )(parent, tile, col_map)


def live_here(live_ref, local):
    return live_ref[lax.axis_index("front")] - lax.axis_index("rows") * local


def own_gram_kernel(live_ref, own_ref, out_ref, hi_ref, lo_ref):
    local, width = own_ref.shape
    rows = lax.broadcasted_iota(jnp.int32, own_ref.shape, 0)
    own = jnp.where(rows < live_here(live_ref, local), own_ref[...], F32(0))
    hi_ref[...], lo_ref[...] = split(own)
    at = 0
    for i in range(width // LB):
        left = slice(i * LB, (i + 1) * LB)
        right = slice(i * LB, width)
        strip = dot3(
            (hi_ref[:, left], lo_ref[:, left]), (hi_ref[:, right], lo_ref[:, right]), TN
        )
        for j in range(strip.shape[1] // LB):
            out_ref[at : at + LB, :] = strip[:, j * LB : (j + 1) * LB]
            at += LB


def own_gram(live_rows, own):
    width = own.shape[1]
    return pl.pallas_call(
        own_gram_kernel,
        out_shape=jax.ShapeDtypeStruct((len(upper_blocks(width)) * LB, LB), F32),
        in_specs=[SMEM, VMEM],
        out_specs=VMEM,
        scratch_shapes=[pltpu.VMEM(own.shape, jnp.bfloat16)] * 2,
        compiler_params=PARAMS,
        name="own_gram",
    )(live_rows, own)


def packed_rows(at, chip, half):
    quarter = half // 4
    piece = LB // 2
    side, first = divmod(at * LB, half)
    turn = chip % 4
    found = []
    for s in range(2):
        q, inner = divmod(first + s * piece, quarter)
        position = (q + 4 - turn) % 4 if side == 0 else (turn + 4 - q) % 4
        found.append(pl.multiple_of(position * quarter + inner, piece))
    return side, found


CHUNK = 128


def gram_kernel(parent_ref, mine_ref, arrived_ref, keep_ref, send_ref, hi_ref, lo_ref, sum_ref):
    children, rows, width = arrived_ref.shape
    half = keep_ref.shape[0]
    group = lax.axis_index("front")
    core, chip = lax.axis_index("rows") % 2, lax.axis_index("rows") // 2

    def pack(child, count):
        mine = parent_ref[child] == group

        @pl.when(mine)
        def _():
            at = pl.ds(pl.multiple_of(count * rows, rows), rows)
            hi_ref[at, :], lo_ref[at, :] = split(arrived_ref[child])

        return count + mine.astype(jnp.int32)

    count = lax.fori_loop(0, children, pack, jnp.int32(0))
    each = CHUNK // rows
    chunks = (count + each - 1) // each
    empty = jnp.zeros((rows, width), jnp.bfloat16)

    def clear(child, carry):
        at = pl.ds(pl.multiple_of(child * rows, rows), rows)
        hi_ref[at, :] = empty
        lo_ref[at, :] = empty
        return carry

    lax.fori_loop(count, jnp.maximum(chunks, 1) * each, clear, 0)

    def add(chunk, base_ref):
        at_rows = pl.ds(pl.multiple_of(chunk * CHUNK, CHUNK), CHUNK)
        at = 0
        for i in range(width // LB):
            left = slice(i * LB, (i + 1) * LB)
            right = slice(i * LB, width)
            strip = dot3(
                (hi_ref[at_rows, left], lo_ref[at_rows, left]),
                (hi_ref[at_rows, right], lo_ref[at_rows, right]),
                TN,
            )
            for j in range(strip.shape[1] // LB):
                here = slice(at, at + LB)
                sum_ref[here, :] = strip[:, j * LB : (j + 1) * LB] + base_ref[here, :]
                at += LB

    add(0, mine_ref)

    def more(chunk, carry):
        add(chunk, sum_ref)
        return carry

    lax.fori_loop(1, chunks, more, 0)
    piece = LB // 2

    def hand_out(refs):
        for at in range(mine_ref.shape[0] // LB):
            side, first = packed_rows(at, chip, half)
            for s in range(2):
                refs[side][pl.ds(first[s], piece), :] = sum_ref[
                    at * LB + s * piece : at * LB + (s + 1) * piece, :
                ]

    pl.when(core == 0)(lambda: hand_out((keep_ref, send_ref)))
    pl.when(core == 1)(lambda: hand_out((send_ref, keep_ref)))


def add_children(parent, mine, arrived):
    children, rows, width = arrived.shape
    half = jax.ShapeDtypeStruct((mine.shape[0] // 2, LB), F32)
    return pl.pallas_call(
        gram_kernel,
        out_shape=(half, half),
        in_specs=[SMEM, VMEM, VMEM],
        out_specs=(VMEM, VMEM),
        scratch_shapes=[pltpu.VMEM((children * rows, width), jnp.bfloat16)] * 2
        + [pltpu.VMEM(mine.shape, F32)],
        compiler_params=PARAMS,
        name="add_children",
    )(parent, mine, arrived)


def row8(x, i):
    return jnp.broadcast_to(x[i : i + 1, :], (8, LB))


def lane8(x, j):
    return jnp.broadcast_to(x[:, j : j + 1], (8, LB))


def total8(terms):
    while len(terms) > 1:
        terms = [terms[i] + terms[i + 1] for i in range(0, len(terms), 2)]
    return terms[0]


def factor_block(slabs):
    count, panel, ahead = len(slabs), 4, 2
    sub = lax.broadcasted_iota(jnp.int32, (8, LB), 0)
    lane = lax.broadcasted_iota(jnp.int32, (8, LB), 1)
    slabs = list(slabs)
    r_out, inv_out = [], []
    here = [jnp.maximum(lane8(slabs[0], j), F32(-3e38)) for j in range(8)]
    for p in range(0, count, panel):
        end = p + panel
        reach = min(end + ahead, count)
        for b in range(p, end):
            a = [[row8(here[j], i) if i <= j else None for j in range(8)] for i in range(8)]
            row = sub + 8 * b
            joined = slabs[b] + jnp.where(lane == row, F32(1), F32(0))
            r = [row8(joined, i) for i in range(8)]
            rd = [None] * 8
            m = [[None] * 8 for _ in range(8)]
            vectors = [r]
            if b + 1 < reach:
                c = [lane8(slabs[b + 1], 8 * b + j) for j in range(8)]
                here = [lane8(slabs[b + 1], 8 * (b + 1) + j) for j in range(8)]
                vectors.append(c)
            for k in range(8):
                rd[k] = 1.0 / a[k][k]
                for j in range(k + 1, 8):
                    m[k][j] = a[k][j] * rd[k]
                    for i in range(j, 8):
                        a[j][i] = a[j][i] - m[k][j] * a[k][i]
                    for vector in vectors:
                        vector[j] = vector[j] - m[k][j] * vector[k]
            pivots, rows = a[0][0], r[0]
            for k in range(1, 8):
                pivots = jnp.where(sub == k, a[k][k], pivots)
                rows = jnp.where(sub == k, r[k], rows)
            rs = lax.rsqrt(pivots)
            rows = rows * rs
            r_out.append(
                jnp.where(lane > row, rows, jnp.where(lane == row, pivots * rs, F32(0)))
            )
            inv_out.append(jnp.where(lane < row, rows, jnp.where(lane == row, rs, F32(0))))
            if b + 1 == reach:
                continue
            u = [c[j] * rd[j] for j in range(8)]
            for j in range(8):
                slabs[b + 1] = slabs[b + 1] - u[j] * r[j]
            for j in range(8):
                for k in range(8):
                    here[j] = here[j] - u[k] * row8(c[k], j)
            if b + 2 == reach:
                continue
            z = [None] * 8
            for k in reversed(range(8)):
                z[k] = r[k] * rd[k]
                for i in range(k + 1, 8):
                    z[k] = z[k] - m[k][i] * z[i]
            for v in range(b + 2, reach):
                cv = [lane8(slabs[v], 8 * b + j) for j in range(8)]
                slabs[v] = slabs[v] - total8([cv[j] * z[j] for j in range(8)])
        if reach < count:
            both = [jnp.where(lane >= 8 * end, r_out[v], inv_out[v]) for v in range(p, end)]
            hi, lo = split(jnp.concatenate(both, axis=0))
            taken = dot(
                jnp.concatenate([hi, hi, lo], axis=0), jnp.concatenate([hi, lo, hi], axis=0), TN
            )
            dead = (lane >= 8 * p) & (lane < 8 * end)
            for v in range(reach, count):
                slabs[v] = jnp.where(dead, F32(0), slabs[v]) - taken[8 * v : 8 * v + 8, :]
    return r_out, inv_out


def tall(a, axis):
    return jnp.concatenate([a[0], a[0], a[1]], axis=axis)


def wide(b, axis):
    return jnp.concatenate([b[0], b[1], b[0]], axis=axis)


def product(a, b, dims):
    return dot(tall(a, dims[0][0]), wide(b, dims[1][0]), dims)


def factor_kernel(
    total_rows, live_ref, mine_ref, other_ref, own_ref, r_ref, q_ref,
    a_ref, inv_ref, strip_ref, q_now_ref,
):
    local, width = own_ref.shape
    n = width // LB
    half = mine_ref.shape[0]
    place = lax.axis_index("rows")
    core, chip = place % 2, place // 2
    diag = lax.broadcasted_iota(jnp.int32, (LB, LB), 0) == lax.broadcasted_iota(
        jnp.int32, (LB, LB), 1
    )
    blocks = upper_blocks(width)

    def fetch(at):
        side, rows = packed_rows(at, chip, half)
        parts = [
            jnp.where(
                core == side, mine_ref[pl.ds(o, LB // 2), :], other_ref[pl.ds(o, LB // 2), :]
            )
            for o in rows
        ]
        return jnp.concatenate(parts, axis=0)

    across, down = [], []
    for i in range(n):
        only = jnp.where(diag, fetch(blocks.index((i, i))), F32(0))
        across.append(
            lax.rsqrt(jnp.sum(only, axis=0, keepdims=True) / total_rows + F32(1e-6))
        )
        down.append(lax.rsqrt(jnp.sum(only, axis=1, keepdims=True) / total_rows + F32(1e-6)))
    root = 2.0 ** ((total_rows.bit_length() - 1) // 2)
    down = [x * F32(1 / root**2) for x in down]
    shift = jnp.where(diag, F32(0.25 * total_rows / root**2), F32(0))

    def scaled(at):
        i, j = blocks[at]
        block = fetch(at) * down[i] * across[j]
        return block + shift if i == j else block

    def unpack():
        for at, (i, j) in enumerate(blocks):
            if at > 0:
                a_ref[i * LB : (i + 1) * LB, j * LB : (j + 1) * LB] = scaled(at)
        rows = lax.broadcasted_iota(jnp.int32, (local, LB), 0)
        live = live_here(live_ref, local)
        for j in range(n):
            cols = slice(j * LB, (j + 1) * LB)
            q_ref[:, cols] = jnp.where(
                rows < live, own_ref[:, cols] * (across[j] * F32(1 / root)), F32(0)
            )

    def take_strip(first):
        left = first * LB
        old = split(strip_ref[...])
        old_tall, old_wide = tall(old, 0), wide(old, 0)
        for i in range(first, n):
            at = slice(i * LB, (i + 1) * LB)
            a_ref[at, i * LB :] = a_ref[at, i * LB :] - dot(
                old_tall[:, at], old_wide[:, i * LB :], TN
            )
        q_ref[:, left:] = q_ref[:, left:] - dot(
            tall(split(q_now_ref[...]), 1), old_wide[:, left:], NN
        )

    def step(first, k, carry):
        o = pl.multiple_of(k * LB, LB)
        if first is None:
            left = 0
            block = scaled(0)
            slabs = [block[8 * v : 8 * v + 8, :] for v in range(LB // 8)]
            unpack()
        else:
            left = first * LB
            slabs = [a_ref[pl.ds(o + 8 * v, 8), pl.ds(o, LB)] for v in range(LB // 8)]
            take_strip(first)
        r_rows, inv_rows = factor_block(slabs)
        for v in range(LB // 8):
            inv_ref[8 * v : 8 * v + 8, :] = inv_rows[v]
        inv = split(inv_ref[...])
        strip = product(inv, split(a_ref[pl.ds(o, LB), left:]), NN)
        column = lax.broadcasted_iota(jnp.int32, strip.shape, 1) + left
        strip = jnp.where(column >= o + LB, strip, F32(0))
        strip_ref[:, left:] = strip
        a_ref[pl.ds(o, LB), left:] = strip
        for v in range(LB // 8):
            a_ref[pl.ds(o + 8 * v, 8), pl.ds(o, LB)] = r_rows[v]
        after = pl.multiple_of(jnp.minimum(k + 1, n - 1) * LB, LB)
        new = split(strip_ref[:, pl.ds(after, LB)])
        a_ref[pl.ds(after, LB), pl.ds(after, LB)] = a_ref[
            pl.ds(after, LB), pl.ds(after, LB)
        ] - product(new, new, TN)
        q_now = product(split(q_ref[:, pl.ds(o, LB)]), inv, NT)
        q_now_ref[...] = q_now
        q_ref[:, pl.ds(o, LB)] = q_now
        return carry

    step(None, jnp.int32(0), 0)
    lax.fori_loop(1, n // 2, functools.partial(step, 0), 0)
    lax.fori_loop(n // 2, n, functools.partial(step, n // 2), 0)
    start = pl.multiple_of(place * r_ref.shape[0], r_ref.shape[0])
    mine = a_ref[pl.ds(start, r_ref.shape[0]), :]
    row = start + lax.broadcasted_iota(jnp.int32, mine.shape, 0)
    column = lax.broadcasted_iota(jnp.int32, mine.shape, 1)
    r_ref[...] = jnp.where(column >= row, mine * F32(root), F32(0))


def factor(live_rows, mine, other, own, out_rows, total_rows):
    local, width = own.shape
    return pl.pallas_call(
        functools.partial(factor_kernel, total_rows),
        out_shape=(
            jax.ShapeDtypeStruct((out_rows, width), F32),
            jax.ShapeDtypeStruct(own.shape, F32),
        ),
        in_specs=[SMEM, VMEM, VMEM, VMEM],
        out_specs=(VMEM, VMEM),
        scratch_shapes=[
            pltpu.VMEM((width, width), F32),
            pltpu.VMEM((LB, LB), F32),
            pltpu.VMEM((LB, width), F32),
            pltpu.VMEM((local, LB), F32),
        ],
        compiler_params=PARAMS,
        name="factor",
    )(live_rows, mine, other, own)


def to_chip(x, k):
    devices = lax.axis_size("rows")
    pairs = [(i, (i + (2 * k if i % 2 == 0 else -2 * k)) % devices) for i in range(devices)]
    return lax.ppermute(x, "rows", pairs)


def to_core(x):
    return lax.ppermute(x, "rows", [(i, i ^ 1) for i in range(lax.axis_size("rows"))])


def sum_over_rows(keep, send):
    chips = lax.axis_size("rows") // 2
    classes = [
        [2 * (a + 4 * i) + c for i in range(chips // 4)] for c in range(2) for a in range(4)
    ]
    quarter = keep.shape[0] // 4
    got = to_core(send)
    part = [
        keep[k * quarter : (k + 1) * quarter] + got[k * quarter : (k + 1) * quarter]
        for k in range(4)
    ]
    far = to_chip(part[2], -2)
    summed = part[0] + to_chip(part[1], 1) + to_chip(part[3], -1) + far
    pieces = lax.all_to_all(
        summed, "rows", split_axis=0, concat_axis=0, axis_index_groups=classes, tiled=True
    )
    done = jnp.sum(pieces.reshape(chips // 4, -1, LB), axis=0)
    whole = lax.all_gather(done, "rows", axis=0, axis_index_groups=classes, tiled=True)
    right = to_chip(whole, -1)
    left = to_chip(whole, 1)
    far = to_chip(right, -1)
    mine = jnp.concatenate([whole, right, far, left])
    return mine, to_core(mine)


def body(own_rows, child_tile, col_map, parent, live_rows):
    own, tile = own_rows[0], child_tile[0]
    arrived = lax.all_to_all(
        place_child(parent, tile, col_map), "front", split_axis=0, concat_axis=0, tiled=True
    )
    keep, send = add_children(parent, own_gram(live_rows, own), arrived)
    mine, other = sum_over_rows(keep, send)
    total_rows = own.shape[0] * lax.axis_size("rows")
    r_rows, panel = factor(live_rows, mine, other, own, tile.shape[0], total_rows)
    return (r_rows[None], panel[None])


def solution(mesh):
    placed = (P("front", "rows", None), P("front", "rows", None), P(), P(), P())
    return jax.shard_map(
        body,
        mesh=mesh,
        in_specs=placed,
        out_specs=(P("front", "rows", None), P("front", "rows", None)),
        check_vma=False,
    )
```

```python
import functools

import jax
import jax.numpy as jnp
from jax import lax
from jax.experimental import pallas as pl
from jax.experimental.pallas import tpu as pltpu
from jax.sharding import PartitionSpec as P

F32 = jnp.float32
LB = 128
NN = ((1,), (0,))
TN = ((0,), (0,))
NT = ((1,), (1,))
VMEM = pl.BlockSpec(memory_space=pltpu.VMEM)
SMEM = pl.BlockSpec(memory_space=pltpu.SMEM)
HBM = pl.BlockSpec(memory_space=pltpu.HBM)
PARAMS = pltpu.CompilerParams(vmem_limit_bytes=32 << 20)


def split(x):
    hi = x.astype(jnp.bfloat16)
    lo = (x - hi.astype(F32)).astype(jnp.bfloat16)
    return hi, lo


def dot(a, b, dims):
    return lax.dot_general(a, b, (dims, ((), ())), preferred_element_type=F32)


def dot3(a, b, dims):
    return dot(a[0], b[0], dims) + (dot(a[0], b[1], dims) + dot(a[1], b[0], dims))


def upper_blocks(width):
    n = width // LB
    return [(i, j) for i in range(n) for j in range(i, n)]


def place_kernel(
    parent_hbm, tile_hbm, map_hbm, out_ref, parent_ref, tile_ref, map_ref, moved_ref, sems
):
    rows, width = tile_ref.shape
    group = lax.axis_index("front")
    fetches = [
        pltpu.make_async_copy(tile_hbm, tile_ref, sems.at[0]),
        pltpu.make_async_copy(map_hbm, map_ref, sems.at[1]),
        pltpu.make_async_copy(parent_hbm, parent_ref, sems.at[3]),
    ]
    for fetch in fetches:
        fetch.start()
    for fetch in fetches:
        fetch.wait()
    tile = tile_ref[...]
    first = tile.astype(jnp.bfloat16)
    rest = tile - first.astype(F32)
    second = rest.astype(jnp.bfloat16)
    third = (rest - second.astype(F32)).astype(jnp.bfloat16)
    parts = jnp.concatenate([first, second, third], axis=0)
    columns = map_ref[pl.ds(group, 1), :]
    for i in range(width // LB):
        target = lax.broadcasted_iota(jnp.int32, (LB, width), 0) + i * LB
        onehot = (target == columns).astype(F32).astype(jnp.bfloat16)
        moved = dot(parts, onehot, NT)
        moved_ref[:, i * LB : (i + 1) * LB] = (
            moved[:rows] + moved[rows : 2 * rows] + moved[2 * rows :]
        )
    copy = pltpu.make_async_copy(moved_ref, out_ref.at[parent_ref[group]], sems.at[2])
    copy.start()
    copy.wait()


def place_child(parent, tile, col_map):
    return pl.pallas_call(
        place_kernel,
        out_shape=jax.ShapeDtypeStruct((col_map.shape[0],) + tile.shape, F32),
        in_specs=[HBM, HBM, HBM],
        out_specs=HBM,
        scratch_shapes=[
            pltpu.SMEM(parent.shape, jnp.int32),
            pltpu.VMEM(tile.shape, F32),
            pltpu.VMEM(col_map.shape, jnp.int32),
            pltpu.VMEM(tile.shape, F32),
            pltpu.SemaphoreType.DMA((4,)),
        ],
        compiler_params=PARAMS,
        name="place_child",
    )(parent, tile, col_map)


def live_here(live_ref, local):
    return live_ref[lax.axis_index("front")] - lax.axis_index("rows") * local


def own_gram_kernel(live_ref, own_ref, out_ref, hi_ref, lo_ref):
    local, width = own_ref.shape
    rows = lax.broadcasted_iota(jnp.int32, own_ref.shape, 0)
    own = jnp.where(rows < live_here(live_ref, local), own_ref[...], F32(0))
    hi_ref[...], lo_ref[...] = split(own)
    at = 0
    for i in range(width // LB):
        left = slice(i * LB, (i + 1) * LB)
        right = slice(i * LB, width)
        strip = dot3(
            (hi_ref[:, left], lo_ref[:, left]), (hi_ref[:, right], lo_ref[:, right]), TN
        )
        for j in range(strip.shape[1] // LB):
            out_ref[at : at + LB, :] = strip[:, j * LB : (j + 1) * LB]
            at += LB


def own_gram(live_rows, own):
    width = own.shape[1]
    return pl.pallas_call(
        own_gram_kernel,
        out_shape=jax.ShapeDtypeStruct((len(upper_blocks(width)) * LB, LB), F32),
        in_specs=[SMEM, VMEM],
        out_specs=VMEM,
        scratch_shapes=[pltpu.VMEM(own.shape, jnp.bfloat16)] * 2,
        compiler_params=PARAMS,
        name="own_gram",
    )(live_rows, own)


def packed_rows(at, chip, half):
    quarter = half // 4
    piece = LB // 2
    side, first = divmod(at * LB, half)
    turn = chip % 4
    found = []
    for s in range(2):
        q, inner = divmod(first + s * piece, quarter)
        position = (q + 4 - turn) % 4 if side == 0 else (turn + 4 - q) % 4
        found.append(pl.multiple_of(position * quarter + inner, piece))
    return side, found


CHUNK = 128


def gram_kernel(parent_ref, mine_ref, arrived_ref, keep_ref, send_ref, hi_ref, lo_ref, sum_ref):
    children, rows, width = arrived_ref.shape
    half = keep_ref.shape[0]
    group = lax.axis_index("front")
    core, chip = lax.axis_index("rows") % 2, lax.axis_index("rows") // 2

    def pack(child, count):
        mine = parent_ref[child] == group

        @pl.when(mine)
        def _():
            at = pl.ds(pl.multiple_of(count * rows, rows), rows)
            hi_ref[at, :], lo_ref[at, :] = split(arrived_ref[child])

        return count + mine.astype(jnp.int32)

    count = lax.fori_loop(0, children, pack, jnp.int32(0))
    each = CHUNK // rows
    chunks = (count + each - 1) // each
    empty = jnp.zeros((rows, width), jnp.bfloat16)

    def clear(child, carry):
        at = pl.ds(pl.multiple_of(child * rows, rows), rows)
        hi_ref[at, :] = empty
        lo_ref[at, :] = empty
        return carry

    lax.fori_loop(count, jnp.maximum(chunks, 1) * each, clear, 0)

    def add(chunk, base_ref):
        at_rows = pl.ds(pl.multiple_of(chunk * CHUNK, CHUNK), CHUNK)
        at = 0
        for i in range(width // LB):
            left = slice(i * LB, (i + 1) * LB)
            right = slice(i * LB, width)
            strip = dot3(
                (hi_ref[at_rows, left], lo_ref[at_rows, left]),
                (hi_ref[at_rows, right], lo_ref[at_rows, right]),
                TN,
            )
            for j in range(strip.shape[1] // LB):
                here = slice(at, at + LB)
                sum_ref[here, :] = strip[:, j * LB : (j + 1) * LB] + base_ref[here, :]
                at += LB

    add(0, mine_ref)

    def more(chunk, carry):
        add(chunk, sum_ref)
        return carry

    lax.fori_loop(1, chunks, more, 0)
    piece = LB // 2

    def hand_out(refs):
        for at in range(mine_ref.shape[0] // LB):
            side, first = packed_rows(at, chip, half)
            for s in range(2):
                refs[side][pl.ds(first[s], piece), :] = sum_ref[
                    at * LB + s * piece : at * LB + (s + 1) * piece, :
                ]

    pl.when(core == 0)(lambda: hand_out((keep_ref, send_ref)))
    pl.when(core == 1)(lambda: hand_out((send_ref, keep_ref)))


def add_children(parent, mine, arrived):
    children, rows, width = arrived.shape
    half = jax.ShapeDtypeStruct((mine.shape[0] // 2, LB), F32)
    return pl.pallas_call(
        gram_kernel,
        out_shape=(half, half),
        in_specs=[SMEM, VMEM, VMEM],
        out_specs=(VMEM, VMEM),
        scratch_shapes=[pltpu.VMEM((children * rows, width), jnp.bfloat16)] * 2
        + [pltpu.VMEM(mine.shape, F32)],
        compiler_params=PARAMS,
        name="add_children",
    )(parent, mine, arrived)


def row8(x, i):
    return jnp.broadcast_to(x[i : i + 1, :], (8, LB))


def lane8(x, j):
    return jnp.broadcast_to(x[:, j : j + 1], (8, LB))


def total8(terms):
    while len(terms) > 1:
        terms = [terms[i] + terms[i + 1] for i in range(0, len(terms), 2)]
    return terms[0]


def factor_block(slabs):
    count, panel, ahead = len(slabs), 4, 2
    sub = lax.broadcasted_iota(jnp.int32, (8, LB), 0)
    lane = lax.broadcasted_iota(jnp.int32, (8, LB), 1)
    slabs = list(slabs)
    r_out, inv_out = [], []
    here = [jnp.maximum(lane8(slabs[0], j), F32(-3e38)) for j in range(8)]
    for p in range(0, count, panel):
        end = p + panel
        reach = min(end + ahead, count)
        for b in range(p, end):
            a = [[row8(here[j], i) if i <= j else None for j in range(8)] for i in range(8)]
            row = sub + 8 * b
            joined = slabs[b] + jnp.where(lane == row, F32(1), F32(0))
            r = [row8(joined, i) for i in range(8)]
            rd = [None] * 8
            m = [[None] * 8 for _ in range(8)]
            vectors = [r]
            if b + 1 < reach:
                c = [lane8(slabs[b + 1], 8 * b + j) for j in range(8)]
                here = [lane8(slabs[b + 1], 8 * (b + 1) + j) for j in range(8)]
                vectors.append(c)
            for k in range(8):
                rd[k] = 1.0 / a[k][k]
                for j in range(k + 1, 8):
                    m[k][j] = a[k][j] * rd[k]
                    for i in range(j, 8):
                        a[j][i] = a[j][i] - m[k][j] * a[k][i]
                    for vector in vectors:
                        vector[j] = vector[j] - m[k][j] * vector[k]
            pivots, rows = a[0][0], r[0]
            for k in range(1, 8):
                pivots = jnp.where(sub == k, a[k][k], pivots)
                rows = jnp.where(sub == k, r[k], rows)
            rs = lax.rsqrt(pivots)
            rows = rows * rs
            r_out.append(
                jnp.where(lane > row, rows, jnp.where(lane == row, pivots * rs, F32(0)))
            )
            inv_out.append(jnp.where(lane < row, rows, jnp.where(lane == row, rs, F32(0))))
            if b + 1 == reach:
                continue
            u = [c[j] * rd[j] for j in range(8)]
            for j in range(8):
                slabs[b + 1] = slabs[b + 1] - u[j] * r[j]
            for j in range(8):
                for k in range(8):
                    here[j] = here[j] - u[k] * row8(c[k], j)
            if b + 2 == reach:
                continue
            z = [None] * 8
            for k in reversed(range(8)):
                z[k] = r[k] * rd[k]
                for i in range(k + 1, 8):
                    z[k] = z[k] - m[k][i] * z[i]
            for v in range(b + 2, reach):
                cv = [lane8(slabs[v], 8 * b + j) for j in range(8)]
                slabs[v] = slabs[v] - total8([cv[j] * z[j] for j in range(8)])
        if reach < count:
            both = [jnp.where(lane >= 8 * end, r_out[v], inv_out[v]) for v in range(p, end)]
            hi, lo = split(jnp.concatenate(both, axis=0))
            taken = dot(
                jnp.concatenate([hi, hi, lo], axis=0), jnp.concatenate([hi, lo, hi], axis=0), TN
            )
            dead = (lane >= 8 * p) & (lane < 8 * end)
            for v in range(reach, count):
                slabs[v] = jnp.where(dead, F32(0), slabs[v]) - taken[8 * v : 8 * v + 8, :]
    return r_out, inv_out


def tall(a, axis):
    return jnp.concatenate([a[0], a[0], a[1]], axis=axis)


def wide(b, axis):
    return jnp.concatenate([b[0], b[1], b[0]], axis=axis)


def product(a, b, dims):
    return dot(tall(a, dims[0][0]), wide(b, dims[1][0]), dims)


def factor_kernel(
    total_rows, live_ref, mine_ref, other_ref, own_ref, r_ref, q_ref,
    a_ref, inv_ref, strip_ref, q_now_ref,
):
    local, width = own_ref.shape
    n = width // LB
    half = mine_ref.shape[0]
    place = lax.axis_index("rows")
    core, chip = place % 2, place // 2
    diag = lax.broadcasted_iota(jnp.int32, (LB, LB), 0) == lax.broadcasted_iota(
        jnp.int32, (LB, LB), 1
    )
    blocks = upper_blocks(width)

    def fetch(at):
        side, rows = packed_rows(at, chip, half)
        parts = [
            jnp.where(
                core == side, mine_ref[pl.ds(o, LB // 2), :], other_ref[pl.ds(o, LB // 2), :]
            )
            for o in rows
        ]
        return jnp.concatenate(parts, axis=0)

    across, down = [], []
    for i in range(n):
        only = jnp.where(diag, fetch(blocks.index((i, i))), F32(0))
        across.append(
            lax.rsqrt(jnp.sum(only, axis=0, keepdims=True) / total_rows + F32(1e-6))
        )
        down.append(lax.rsqrt(jnp.sum(only, axis=1, keepdims=True) / total_rows + F32(1e-6)))
    root = 2.0 ** ((total_rows.bit_length() - 1) // 2)
    down = [x * F32(1 / root**2) for x in down]
    shift = jnp.where(diag, F32(0.25 * total_rows / root**2), F32(0))

    def scaled(at):
        i, j = blocks[at]
        block = fetch(at) * down[i] * across[j]
        return block + shift if i == j else block

    def unpack():
        for at, (i, j) in enumerate(blocks):
            if at > 0:
                a_ref[i * LB : (i + 1) * LB, j * LB : (j + 1) * LB] = scaled(at)
        rows = lax.broadcasted_iota(jnp.int32, (local, LB), 0)
        live = live_here(live_ref, local)
        for j in range(n):
            cols = slice(j * LB, (j + 1) * LB)
            q_ref[:, cols] = jnp.where(
                rows < live, own_ref[:, cols] * (across[j] * F32(1 / root)), F32(0)
            )

    def take_strip(first):
        left = first * LB
        old = split(strip_ref[...])
        old_tall, old_wide = tall(old, 0), wide(old, 0)
        for i in range(first, n):
            at = slice(i * LB, (i + 1) * LB)
            a_ref[at, i * LB :] = a_ref[at, i * LB :] - dot(
                old_tall[:, at], old_wide[:, i * LB :], TN
            )
        q_ref[:, left:] = q_ref[:, left:] - dot(
            tall(split(q_now_ref[...]), 1), old_wide[:, left:], NN
        )

    def step(first, k, carry):
        o = pl.multiple_of(k * LB, LB)
        if first is None:
            left = 0
            block = scaled(0)
            slabs = [block[8 * v : 8 * v + 8, :] for v in range(LB // 8)]
            unpack()
        else:
            left = first * LB
            slabs = [a_ref[pl.ds(o + 8 * v, 8), pl.ds(o, LB)] for v in range(LB // 8)]
            take_strip(first)
        r_rows, inv_rows = factor_block(slabs)
        for v in range(LB // 8):
            inv_ref[8 * v : 8 * v + 8, :] = inv_rows[v]
        inv = split(inv_ref[...])
        strip = product(inv, split(a_ref[pl.ds(o, LB), left:]), NN)
        column = lax.broadcasted_iota(jnp.int32, strip.shape, 1) + left
        strip = jnp.where(column >= o + LB, strip, F32(0))
        strip_ref[:, left:] = strip
        a_ref[pl.ds(o, LB), left:] = strip
        for v in range(LB // 8):
            a_ref[pl.ds(o + 8 * v, 8), pl.ds(o, LB)] = r_rows[v]
        after = pl.multiple_of(jnp.minimum(k + 1, n - 1) * LB, LB)
        new = split(strip_ref[:, pl.ds(after, LB)])
        a_ref[pl.ds(after, LB), pl.ds(after, LB)] = a_ref[
            pl.ds(after, LB), pl.ds(after, LB)
        ] - product(new, new, TN)
        q_now = product(split(q_ref[:, pl.ds(o, LB)]), inv, NT)
        q_now_ref[...] = q_now
        q_ref[:, pl.ds(o, LB)] = q_now
        return carry

    step(None, jnp.int32(0), 0)
    lax.fori_loop(1, n // 2, functools.partial(step, 0), 0)
    lax.fori_loop(n // 2, n, functools.partial(step, n // 2), 0)
    start = pl.multiple_of(place * r_ref.shape[0], r_ref.shape[0])
    mine = a_ref[pl.ds(start, r_ref.shape[0]), :]
    row = start + lax.broadcasted_iota(jnp.int32, mine.shape, 0)
    column = lax.broadcasted_iota(jnp.int32, mine.shape, 1)
    r_ref[...] = jnp.where(column >= row, mine * F32(root), F32(0))


def factor(live_rows, mine, other, own, out_rows, total_rows):
    local, width = own.shape
    return pl.pallas_call(
        functools.partial(factor_kernel, total_rows),
        out_shape=(
            jax.ShapeDtypeStruct((out_rows, width), F32),
            jax.ShapeDtypeStruct(own.shape, F32),
        ),
        in_specs=[SMEM, VMEM, VMEM, VMEM],
        out_specs=(VMEM, VMEM),
        scratch_shapes=[
            pltpu.VMEM((width, width), F32),
            pltpu.VMEM((LB, LB), F32),
            pltpu.VMEM((LB, width), F32),
            pltpu.VMEM((local, LB), F32),
        ],
        compiler_params=PARAMS,
        name="factor",
    )(live_rows, mine, other, own)


def to_chip(x, k):
    devices = lax.axis_size("rows")
    pairs = [(i, (i + (2 * k if i % 2 == 0 else -2 * k)) % devices) for i in range(devices)]
    return lax.ppermute(x, "rows", pairs)


def to_core(x):
    return lax.ppermute(x, "rows", [(i, i ^ 1) for i in range(lax.axis_size("rows"))])


def sum_over_rows(keep, send):
    chips = lax.axis_size("rows") // 2
    classes = [
        [2 * (a + 4 * i) + c for i in range(chips // 4)] for c in range(2) for a in range(4)
    ]
    quarter = keep.shape[0] // 4
    got = to_core(send)
    part = [
        keep[k * quarter : (k + 1) * quarter] + got[k * quarter : (k + 1) * quarter]
        for k in range(4)
    ]
    far = to_chip(part[2], -2)
    summed = part[0] + to_chip(part[1], 1) + to_chip(part[3], -1) + far
    pieces = lax.all_to_all(
        summed, "rows", split_axis=0, concat_axis=0, axis_index_groups=classes, tiled=True
    )
    done = jnp.sum(pieces.reshape(chips // 4, -1, LB), axis=0)
    whole = lax.all_gather(done, "rows", axis=0, axis_index_groups=classes, tiled=True)
    right = to_chip(whole, -1)
    left = to_chip(whole, 1)
    far = to_chip(whole, -2)
    mine = jnp.concatenate([whole, right, far, left])
    return mine, to_core(mine)


def body(own_rows, child_tile, col_map, parent, live_rows):
    own, tile = own_rows[0], child_tile[0]
    arrived = lax.all_to_all(
        place_child(parent, tile, col_map), "front", split_axis=0, concat_axis=0, tiled=True
    )
    keep, send = add_children(parent, own_gram(live_rows, own), arrived)
    mine, other = sum_over_rows(keep, send)
    total_rows = own.shape[0] * lax.axis_size("rows")
    r_rows, panel = factor(live_rows, mine, other, own, tile.shape[0], total_rows)
    return (r_rows[None], panel[None])


def solution(mesh):
    placed = (P("front", "rows", None), P("front", "rows", None), P(), P(), P())
    return jax.shard_map(
        body,
        mesh=mesh,
        in_specs=placed,
        out_specs=(P("front", "rows", None), P("front", "rows", None)),
        check_vma=False,
    )
```

```python
import functools

import jax
import jax.numpy as jnp
from jax import lax
from jax.experimental import pallas as pl
from jax.experimental.pallas import tpu as pltpu
from jax.sharding import PartitionSpec as P

F32 = jnp.float32
LB = 128
NN = ((1,), (0,))
TN = ((0,), (0,))
NT = ((1,), (1,))
VMEM = pl.BlockSpec(memory_space=pltpu.VMEM)
SMEM = pl.BlockSpec(memory_space=pltpu.SMEM)
HBM = pl.BlockSpec(memory_space=pltpu.HBM)
PARAMS = pltpu.CompilerParams(vmem_limit_bytes=32 << 20)


def split(x):
    hi = x.astype(jnp.bfloat16)
    lo = (x - hi.astype(F32)).astype(jnp.bfloat16)
    return hi, lo


def dot(a, b, dims):
    return lax.dot_general(a, b, (dims, ((), ())), preferred_element_type=F32)


def dot3(a, b, dims):
    return dot(a[0], b[0], dims) + (dot(a[0], b[1], dims) + dot(a[1], b[0], dims))


def upper_blocks(width):
    n = width // LB
    return [(i, j) for i in range(n) for j in range(i, n)]


def place_kernel(
    parent_hbm, tile_hbm, map_hbm, out_ref, parent_ref, tile_ref, map_ref, moved_ref, sems
):
    rows, width = tile_ref.shape
    group = lax.axis_index("front")
    fetches = [
        pltpu.make_async_copy(tile_hbm, tile_ref, sems.at[0]),
        pltpu.make_async_copy(map_hbm, map_ref, sems.at[1]),
        pltpu.make_async_copy(parent_hbm, parent_ref, sems.at[3]),
    ]
    for fetch in fetches:
        fetch.start()
    for fetch in fetches:
        fetch.wait()
    tile = tile_ref[...]
    first = tile.astype(jnp.bfloat16)
    rest = tile - first.astype(F32)
    second = rest.astype(jnp.bfloat16)
    third = (rest - second.astype(F32)).astype(jnp.bfloat16)
    parts = jnp.concatenate([first, second, third], axis=0)
    columns = map_ref[pl.ds(group, 1), :]
    for i in range(width // LB):
        target = lax.broadcasted_iota(jnp.int32, (LB, width), 0) + i * LB
        onehot = (target == columns).astype(F32).astype(jnp.bfloat16)
        moved = dot(parts, onehot, NT)
        moved_ref[:, i * LB : (i + 1) * LB] = (
            moved[:rows] + moved[rows : 2 * rows] + moved[2 * rows :]
        )
    copy = pltpu.make_async_copy(moved_ref, out_ref.at[parent_ref[group]], sems.at[2])
    copy.start()
    copy.wait()


def place_child(parent, tile, col_map):
    return pl.pallas_call(
        place_kernel,
        out_shape=jax.ShapeDtypeStruct((col_map.shape[0],) + tile.shape, F32),
        in_specs=[HBM, HBM, HBM],
        out_specs=HBM,
        scratch_shapes=[
            pltpu.SMEM(parent.shape, jnp.int32),
            pltpu.VMEM(tile.shape, F32),
            pltpu.VMEM(col_map.shape, jnp.int32),
            pltpu.VMEM(tile.shape, F32),
            pltpu.SemaphoreType.DMA((4,)),
        ],
        compiler_params=pltpu.CompilerParams(vmem_limit_bytes=63 << 20),
        name="place_child",
    )(parent, tile, col_map)


def live_here(live_ref, local):
    return live_ref[lax.axis_index("front")] - lax.axis_index("rows") * local


def own_gram_kernel(live_ref, own_ref, out_ref, hi_ref, lo_ref):
    local, width = own_ref.shape
    rows = lax.broadcasted_iota(jnp.int32, own_ref.shape, 0)
    own = jnp.where(rows < live_here(live_ref, local), own_ref[...], F32(0))
    hi_ref[...], lo_ref[...] = split(own)
    at = 0
    for i in range(width // LB):
        left = slice(i * LB, (i + 1) * LB)
        right = slice(i * LB, width)
        strip = dot3(
            (hi_ref[:, left], lo_ref[:, left]), (hi_ref[:, right], lo_ref[:, right]), TN
        )
        for j in range(strip.shape[1] // LB):
            out_ref[at : at + LB, :] = strip[:, j * LB : (j + 1) * LB]
            at += LB


def own_gram(live_rows, own):
    width = own.shape[1]
    return pl.pallas_call(
        own_gram_kernel,
        out_shape=jax.ShapeDtypeStruct((len(upper_blocks(width)) * LB, LB), F32),
        in_specs=[SMEM, VMEM],
        out_specs=VMEM,
        scratch_shapes=[pltpu.VMEM(own.shape, jnp.bfloat16)] * 2,
        compiler_params=PARAMS,
        name="own_gram",
    )(live_rows, own)


def packed_rows(at, chip, half):
    quarter = half // 4
    piece = LB // 2
    side, first = divmod(at * LB, half)
    turn = chip % 4
    found = []
    for s in range(2):
        q, inner = divmod(first + s * piece, quarter)
        position = (q + 4 - turn) % 4 if side == 0 else (turn + 4 - q) % 4
        found.append(pl.multiple_of(position * quarter + inner, piece))
    return side, found


CHUNK = 128


def gram_kernel(parent_ref, mine_ref, arrived_ref, keep_ref, send_ref, hi_ref, lo_ref, sum_ref):
    children, rows, width = arrived_ref.shape
    half = keep_ref.shape[0]
    group = lax.axis_index("front")
    core, chip = lax.axis_index("rows") % 2, lax.axis_index("rows") // 2

    def pack(child, count):
        mine = parent_ref[child] == group

        @pl.when(mine)
        def _():
            at = pl.ds(pl.multiple_of(count * rows, rows), rows)
            hi_ref[at, :], lo_ref[at, :] = split(arrived_ref[child])

        return count + mine.astype(jnp.int32)

    count = lax.fori_loop(0, children, pack, jnp.int32(0))
    each = CHUNK // rows
    chunks = (count + each - 1) // each
    empty = jnp.zeros((rows, width), jnp.bfloat16)

    def clear(child, carry):
        at = pl.ds(pl.multiple_of(child * rows, rows), rows)
        hi_ref[at, :] = empty
        lo_ref[at, :] = empty
        return carry

    lax.fori_loop(count, jnp.maximum(chunks, 1) * each, clear, 0)

    def add(chunk, base_ref):
        at_rows = pl.ds(pl.multiple_of(chunk * CHUNK, CHUNK), CHUNK)
        at = 0
        for i in range(width // LB):
            left = slice(i * LB, (i + 1) * LB)
            right = slice(i * LB, width)
            strip = dot3(
                (hi_ref[at_rows, left], lo_ref[at_rows, left]),
                (hi_ref[at_rows, right], lo_ref[at_rows, right]),
                TN,
            )
            for j in range(strip.shape[1] // LB):
                here = slice(at, at + LB)
                sum_ref[here, :] = strip[:, j * LB : (j + 1) * LB] + base_ref[here, :]
                at += LB

    add(0, mine_ref)

    def more(chunk, carry):
        add(chunk, sum_ref)
        return carry

    lax.fori_loop(1, chunks, more, 0)
    piece = LB // 2

    def hand_out(refs):
        for at in range(mine_ref.shape[0] // LB):
            side, first = packed_rows(at, chip, half)
            for s in range(2):
                refs[side][pl.ds(first[s], piece), :] = sum_ref[
                    at * LB + s * piece : at * LB + (s + 1) * piece, :
                ]

    pl.when(core == 0)(lambda: hand_out((keep_ref, send_ref)))
    pl.when(core == 1)(lambda: hand_out((send_ref, keep_ref)))


def add_children(parent, mine, arrived):
    children, rows, width = arrived.shape
    half = jax.ShapeDtypeStruct((mine.shape[0] // 2, LB), F32)
    return pl.pallas_call(
        gram_kernel,
        out_shape=(half, half),
        in_specs=[SMEM, VMEM, VMEM],
        out_specs=(VMEM, VMEM),
        scratch_shapes=[pltpu.VMEM((children * rows, width), jnp.bfloat16)] * 2
        + [pltpu.VMEM(mine.shape, F32)],
        compiler_params=PARAMS,
        name="add_children",
    )(parent, mine, arrived)


def row8(x, i):
    return jnp.broadcast_to(x[i : i + 1, :], (8, LB))


def lane8(x, j):
    return jnp.broadcast_to(x[:, j : j + 1], (8, LB))


def total8(terms):
    while len(terms) > 1:
        terms = [terms[i] + terms[i + 1] for i in range(0, len(terms), 2)]
    return terms[0]


def factor_block(slabs):
    count, panel, ahead = len(slabs), 4, 2
    sub = lax.broadcasted_iota(jnp.int32, (8, LB), 0)
    lane = lax.broadcasted_iota(jnp.int32, (8, LB), 1)
    slabs = list(slabs)
    r_out, inv_out = [], []
    here = [jnp.maximum(lane8(slabs[0], j), F32(-3e38)) for j in range(8)]
    for p in range(0, count, panel):
        end = p + panel
        reach = min(end + ahead, count)
        for b in range(p, end):
            a = [[row8(here[j], i) if i <= j else None for j in range(8)] for i in range(8)]
            row = sub + 8 * b
            joined = slabs[b] + jnp.where(lane == row, F32(1), F32(0))
            r = [row8(joined, i) for i in range(8)]
            rd = [None] * 8
            m = [[None] * 8 for _ in range(8)]
            vectors = [r]
            if b + 1 < reach:
                c = [lane8(slabs[b + 1], 8 * b + j) for j in range(8)]
                here = [lane8(slabs[b + 1], 8 * (b + 1) + j) for j in range(8)]
                vectors.append(c)
            for k in range(8):
                rd[k] = 1.0 / a[k][k]
                for j in range(k + 1, 8):
                    m[k][j] = a[k][j] * rd[k]
                    for i in range(j, 8):
                        a[j][i] = a[j][i] - m[k][j] * a[k][i]
                    for vector in vectors:
                        vector[j] = vector[j] - m[k][j] * vector[k]
            pivots, rows = a[0][0], r[0]
            for k in range(1, 8):
                pivots = jnp.where(sub == k, a[k][k], pivots)
                rows = jnp.where(sub == k, r[k], rows)
            rs = lax.rsqrt(pivots)
            rows = rows * rs
            r_out.append(
                jnp.where(lane > row, rows, jnp.where(lane == row, pivots * rs, F32(0)))
            )
            inv_out.append(jnp.where(lane < row, rows, jnp.where(lane == row, rs, F32(0))))
            if b + 1 == reach:
                continue
            u = [c[j] * rd[j] for j in range(8)]
            for j in range(8):
                slabs[b + 1] = slabs[b + 1] - u[j] * r[j]
            for j in range(8):
                for k in range(8):
                    here[j] = here[j] - u[k] * row8(c[k], j)
            if b + 2 == reach:
                continue
            z = [None] * 8
            for k in reversed(range(8)):
                z[k] = r[k] * rd[k]
                for i in range(k + 1, 8):
                    z[k] = z[k] - m[k][i] * z[i]
            for v in range(b + 2, reach):
                cv = [lane8(slabs[v], 8 * b + j) for j in range(8)]
                slabs[v] = slabs[v] - total8([cv[j] * z[j] for j in range(8)])
        if reach < count:
            both = [jnp.where(lane >= 8 * end, r_out[v], inv_out[v]) for v in range(p, end)]
            hi, lo = split(jnp.concatenate(both, axis=0))
            taken = dot(
                jnp.concatenate([hi, hi, lo], axis=0), jnp.concatenate([hi, lo, hi], axis=0), TN
            )
            dead = (lane >= 8 * p) & (lane < 8 * end)
            for v in range(reach, count):
                slabs[v] = jnp.where(dead, F32(0), slabs[v]) - taken[8 * v : 8 * v + 8, :]
    return r_out, inv_out


def tall(a, axis):
    return jnp.concatenate([a[0], a[0], a[1]], axis=axis)


def wide(b, axis):
    return jnp.concatenate([b[0], b[1], b[0]], axis=axis)


def product(a, b, dims):
    return dot(tall(a, dims[0][0]), wide(b, dims[1][0]), dims)


def factor_kernel(
    total_rows, live_ref, mine_ref, other_ref, own_ref, r_ref, q_ref,
    a_ref, inv_ref, strip_ref, q_now_ref,
):
    local, width = own_ref.shape
    n = width // LB
    half = mine_ref.shape[0]
    place = lax.axis_index("rows")
    core, chip = place % 2, place // 2
    diag = lax.broadcasted_iota(jnp.int32, (LB, LB), 0) == lax.broadcasted_iota(
        jnp.int32, (LB, LB), 1
    )
    blocks = upper_blocks(width)

    def fetch(at):
        side, rows = packed_rows(at, chip, half)
        parts = [
            jnp.where(
                core == side, mine_ref[pl.ds(o, LB // 2), :], other_ref[pl.ds(o, LB // 2), :]
            )
            for o in rows
        ]
        return jnp.concatenate(parts, axis=0)

    across, down = [], []
    for i in range(n):
        only = jnp.where(diag, fetch(blocks.index((i, i))), F32(0))
        across.append(
            lax.rsqrt(jnp.sum(only, axis=0, keepdims=True) / total_rows + F32(1e-6))
        )
        down.append(lax.rsqrt(jnp.sum(only, axis=1, keepdims=True) / total_rows + F32(1e-6)))
    root = 2.0 ** ((total_rows.bit_length() - 1) // 2)
    down = [x * F32(1 / root**2) for x in down]
    shift = jnp.where(diag, F32(0.25 * total_rows / root**2), F32(0))

    def scaled(at):
        i, j = blocks[at]
        block = fetch(at) * down[i] * across[j]
        return block + shift if i == j else block

    def unpack():
        for at, (i, j) in enumerate(blocks):
            if at > 0:
                a_ref[i * LB : (i + 1) * LB, j * LB : (j + 1) * LB] = scaled(at)
        rows = lax.broadcasted_iota(jnp.int32, (local, LB), 0)
        live = live_here(live_ref, local)
        for j in range(n):
            cols = slice(j * LB, (j + 1) * LB)
            q_ref[:, cols] = jnp.where(
                rows < live, own_ref[:, cols] * (across[j] * F32(1 / root)), F32(0)
            )

    def take_strip(first):
        left = first * LB
        old = split(strip_ref[...])
        old_tall, old_wide = tall(old, 0), wide(old, 0)
        for i in range(first, n):
            at = slice(i * LB, (i + 1) * LB)
            a_ref[at, i * LB :] = a_ref[at, i * LB :] - dot(
                old_tall[:, at], old_wide[:, i * LB :], TN
            )
        q_ref[:, left:] = q_ref[:, left:] - dot(
            tall(split(q_now_ref[...]), 1), old_wide[:, left:], NN
        )

    def step(first, k, carry):
        o = pl.multiple_of(k * LB, LB)
        if first is None:
            left = 0
            block = scaled(0)
            slabs = [block[8 * v : 8 * v + 8, :] for v in range(LB // 8)]
            unpack()
        else:
            left = first * LB
            slabs = [a_ref[pl.ds(o + 8 * v, 8), pl.ds(o, LB)] for v in range(LB // 8)]
            take_strip(first)
        r_rows, inv_rows = factor_block(slabs)
        for v in range(LB // 8):
            inv_ref[8 * v : 8 * v + 8, :] = inv_rows[v]
        inv = split(inv_ref[...])
        strip = product(inv, split(a_ref[pl.ds(o, LB), left:]), NN)
        column = lax.broadcasted_iota(jnp.int32, strip.shape, 1) + left
        strip = jnp.where(column >= o + LB, strip, F32(0))
        strip_ref[:, left:] = strip
        a_ref[pl.ds(o, LB), left:] = strip
        for v in range(LB // 8):
            a_ref[pl.ds(o + 8 * v, 8), pl.ds(o, LB)] = r_rows[v]
        after = pl.multiple_of(jnp.minimum(k + 1, n - 1) * LB, LB)
        new = split(strip_ref[:, pl.ds(after, LB)])
        a_ref[pl.ds(after, LB), pl.ds(after, LB)] = a_ref[
            pl.ds(after, LB), pl.ds(after, LB)
        ] - product(new, new, TN)
        q_now = product(split(q_ref[:, pl.ds(o, LB)]), inv, NT)
        q_now_ref[...] = q_now
        q_ref[:, pl.ds(o, LB)] = q_now
        return carry

    step(None, jnp.int32(0), 0)
    lax.fori_loop(1, n // 2, functools.partial(step, 1), 0)
    lax.fori_loop(n // 2, n, functools.partial(step, n // 2), 0)
    start = pl.multiple_of(place * r_ref.shape[0], r_ref.shape[0])
    mine = a_ref[pl.ds(start, r_ref.shape[0]), :]
    row = start + lax.broadcasted_iota(jnp.int32, mine.shape, 0)
    column = lax.broadcasted_iota(jnp.int32, mine.shape, 1)
    r_ref[...] = jnp.where(column >= row, mine * F32(root), F32(0))


def factor(live_rows, mine, other, own, out_rows, total_rows):
    local, width = own.shape
    return pl.pallas_call(
        functools.partial(factor_kernel, total_rows),
        out_shape=(
            jax.ShapeDtypeStruct((out_rows, width), F32),
            jax.ShapeDtypeStruct(own.shape, F32),
        ),
        in_specs=[SMEM, VMEM, VMEM, VMEM],
        out_specs=(VMEM, VMEM),
        scratch_shapes=[
            pltpu.VMEM((width, width), F32),
            pltpu.VMEM((LB, LB), F32),
            pltpu.VMEM((LB, width), F32),
            pltpu.VMEM((local, LB), F32),
        ],
        compiler_params=PARAMS,
        name="factor",
    )(live_rows, mine, other, own)


def to_chip(x, k):
    devices = lax.axis_size("rows")
    pairs = [(i, (i + (2 * k if i % 2 == 0 else -2 * k)) % devices) for i in range(devices)]
    return lax.ppermute(x, "rows", pairs)


def to_core(x):
    return lax.ppermute(x, "rows", [(i, i ^ 1) for i in range(lax.axis_size("rows"))])


def sum_over_rows(keep, send):
    chips = lax.axis_size("rows") // 2
    classes = [
        [2 * (a + 4 * i) + c for i in range(chips // 4)] for c in range(2) for a in range(4)
    ]
    quarter = keep.shape[0] // 4
    got = to_core(send)
    part = [
        keep[k * quarter : (k + 1) * quarter] + got[k * quarter : (k + 1) * quarter]
        for k in range(4)
    ]
    far = to_chip(part[2], -2)
    summed = part[0] + to_chip(part[1], 1) + to_chip(part[3], -1) + far
    pieces = lax.all_to_all(
        summed, "rows", split_axis=0, concat_axis=0, axis_index_groups=classes, tiled=True
    )
    done = jnp.sum(pieces.reshape(chips // 4, -1, LB), axis=0)
    whole = lax.all_gather(done, "rows", axis=0, axis_index_groups=classes, tiled=True)
    right = to_chip(whole, -1)
    left = to_chip(whole, 1)
    far = to_chip(whole, -2)
    mine = jnp.concatenate([whole, right, far, left])
    return mine, to_core(mine)


def body(own_rows, child_tile, col_map, parent, live_rows):
    own, tile = own_rows[0], child_tile[0]
    arrived = lax.all_to_all(
        place_child(parent, tile, col_map), "front", split_axis=0, concat_axis=0, tiled=True
    )
    keep, send = add_children(parent, own_gram(live_rows, own), arrived)
    mine, other = sum_over_rows(keep, send)
    total_rows = own.shape[0] * lax.axis_size("rows")
    r_rows, panel = factor(live_rows, mine, other, own, tile.shape[0], total_rows)
    return (r_rows[None], panel[None])


def solution(mesh):
    placed = (P("front", "rows", None), P("front", "rows", None), P(), P(), P())
    return jax.shard_map(
        body,
        mesh=mesh,
        in_specs=placed,
        out_specs=(P("front", "rows", None), P("front", "rows", None)),
        check_vma=False,
    )
```

```python
import functools

import jax
import jax.numpy as jnp
from jax import lax
from jax.experimental import pallas as pl
from jax.experimental.pallas import tpu as pltpu
from jax.sharding import PartitionSpec as P

F32 = jnp.float32
LB = 128
NN = ((1,), (0,))
TN = ((0,), (0,))
NT = ((1,), (1,))
VMEM = pl.BlockSpec(memory_space=pltpu.VMEM)
SMEM = pl.BlockSpec(memory_space=pltpu.SMEM)
HBM = pl.BlockSpec(memory_space=pltpu.HBM)
PARAMS = pltpu.CompilerParams(vmem_limit_bytes=32 << 20)


def split(x):
    hi = x.astype(jnp.bfloat16)
    lo = (x - hi.astype(F32)).astype(jnp.bfloat16)
    return hi, lo


def dot(a, b, dims):
    return lax.dot_general(a, b, (dims, ((), ())), preferred_element_type=F32)


def dot3(a, b, dims):
    return dot(a[0], b[0], dims) + (dot(a[0], b[1], dims) + dot(a[1], b[0], dims))


def upper_blocks(width):
    n = width // LB
    return [(i, j) for i in range(n) for j in range(i, n)]


def place_kernel(
    parent_hbm, tile_hbm, map_hbm, out_ref, parent_ref, tile_ref, map_ref, moved_ref, sems
):
    rows, width = tile_ref.shape
    group = lax.axis_index("front")
    fetches = [
        pltpu.make_async_copy(tile_hbm, tile_ref, sems.at[0]),
        pltpu.make_async_copy(map_hbm, map_ref, sems.at[1]),
        pltpu.make_async_copy(parent_hbm, parent_ref, sems.at[3]),
    ]
    for fetch in fetches:
        fetch.start()
    for fetch in fetches:
        fetch.wait()
    tile = tile_ref[...]
    first = tile.astype(jnp.bfloat16)
    rest = tile - first.astype(F32)
    second = rest.astype(jnp.bfloat16)
    third = (rest - second.astype(F32)).astype(jnp.bfloat16)
    parts = jnp.concatenate([first, second, third], axis=0)
    columns = map_ref[pl.ds(group, 1), :]
    for i in range(width // LB):
        target = lax.broadcasted_iota(jnp.int32, (LB, width), 0) + i * LB
        onehot = (target == columns).astype(F32).astype(jnp.bfloat16)
        moved = dot(parts, onehot, NT)
        moved_ref[:, i * LB : (i + 1) * LB] = (
            moved[:rows] + moved[rows : 2 * rows] + moved[2 * rows :]
        )
    copy = pltpu.make_async_copy(moved_ref, out_ref.at[parent_ref[group]], sems.at[2])
    copy.start()
    copy.wait()


def place_child(parent, tile, col_map):
    return pl.pallas_call(
        place_kernel,
        out_shape=jax.ShapeDtypeStruct((col_map.shape[0],) + tile.shape, F32),
        in_specs=[HBM, HBM, HBM],
        out_specs=HBM,
        scratch_shapes=[
            pltpu.SMEM(parent.shape, jnp.int32),
            pltpu.VMEM(tile.shape, F32),
            pltpu.VMEM(col_map.shape, jnp.int32),
            pltpu.VMEM(tile.shape, F32),
            pltpu.SemaphoreType.DMA((4,)),
        ],
        compiler_params=pltpu.CompilerParams(vmem_limit_bytes=63 << 20),
        name="place_child",
    )(parent, tile, col_map)


def live_here(live_ref, local):
    return live_ref[lax.axis_index("front")] - lax.axis_index("rows") * local


def own_gram_kernel(live_ref, own_ref, out_ref, hi_ref, lo_ref):
    local, width = own_ref.shape
    rows = lax.broadcasted_iota(jnp.int32, own_ref.shape, 0)
    own = jnp.where(rows < live_here(live_ref, local), own_ref[...], F32(0))
    hi_ref[...], lo_ref[...] = split(own)
    at = 0
    for i in range(width // LB):
        left = slice(i * LB, (i + 1) * LB)
        right = slice(i * LB, width)
        strip = dot3(
            (hi_ref[:, left], lo_ref[:, left]), (hi_ref[:, right], lo_ref[:, right]), TN
        )
        for j in range(strip.shape[1] // LB):
            out_ref[at : at + LB, :] = strip[:, j * LB : (j + 1) * LB]
            at += LB


def own_gram(live_rows, own):
    width = own.shape[1]
    return pl.pallas_call(
        own_gram_kernel,
        out_shape=jax.ShapeDtypeStruct((len(upper_blocks(width)) * LB, LB), F32),
        in_specs=[SMEM, VMEM],
        out_specs=VMEM,
        scratch_shapes=[pltpu.VMEM(own.shape, jnp.bfloat16)] * 2,
        compiler_params=PARAMS,
        name="own_gram",
    )(live_rows, own)


def packed_rows(at, chip, half):
    quarter = half // 4
    piece = LB // 2
    side, first = divmod(at * LB, half)
    turn = chip % 4
    found = []
    for s in range(2):
        q, inner = divmod(first + s * piece, quarter)
        position = (q + 4 - turn) % 4 if side == 0 else (turn + 4 - q) % 4
        found.append(pl.multiple_of(position * quarter + inner, piece))
    return side, found


CHUNK = 128


def gram_kernel(parent_ref, mine_ref, arrived_ref, keep_ref, send_ref, hi_ref, lo_ref, sum_ref):
    children, rows, width = arrived_ref.shape
    half = keep_ref.shape[0]
    group = lax.axis_index("front")
    core, chip = lax.axis_index("rows") % 2, lax.axis_index("rows") // 2

    def pack(child, count):
        mine = parent_ref[child] == group

        @pl.when(mine)
        def _():
            at = pl.ds(pl.multiple_of(count * rows, rows), rows)
            hi_ref[at, :], lo_ref[at, :] = split(arrived_ref[child])

        return count + mine.astype(jnp.int32)

    count = lax.fori_loop(0, children, pack, jnp.int32(0))
    each = CHUNK // rows
    chunks = (count + each - 1) // each
    empty = jnp.zeros((rows, width), jnp.bfloat16)

    def clear(child, carry):
        at = pl.ds(pl.multiple_of(child * rows, rows), rows)
        hi_ref[at, :] = empty
        lo_ref[at, :] = empty
        return carry

    lax.fori_loop(count, jnp.maximum(chunks, 1) * each, clear, 0)

    def add(chunk, base_ref):
        at_rows = pl.ds(pl.multiple_of(chunk * CHUNK, CHUNK), CHUNK)
        at = 0
        for i in range(width // LB):
            left = slice(i * LB, (i + 1) * LB)
            right = slice(i * LB, width)
            strip = dot3(
                (hi_ref[at_rows, left], lo_ref[at_rows, left]),
                (hi_ref[at_rows, right], lo_ref[at_rows, right]),
                TN,
            )
            for j in range(strip.shape[1] // LB):
                here = slice(at, at + LB)
                sum_ref[here, :] = strip[:, j * LB : (j + 1) * LB] + base_ref[here, :]
                at += LB

    add(0, mine_ref)

    def more(chunk, carry):
        add(chunk, sum_ref)
        return carry

    lax.fori_loop(1, chunks, more, 0)
    piece = LB // 2

    def hand_out(refs):
        for at in range(mine_ref.shape[0] // LB):
            side, first = packed_rows(at, chip, half)
            for s in range(2):
                refs[side][pl.ds(first[s], piece), :] = sum_ref[
                    at * LB + s * piece : at * LB + (s + 1) * piece, :
                ]

    pl.when(core == 0)(lambda: hand_out((keep_ref, send_ref)))
    pl.when(core == 1)(lambda: hand_out((send_ref, keep_ref)))


def add_children(parent, mine, arrived):
    children, rows, width = arrived.shape
    half = jax.ShapeDtypeStruct((mine.shape[0] // 2, LB), F32)
    return pl.pallas_call(
        gram_kernel,
        out_shape=(half, half),
        in_specs=[SMEM, VMEM, VMEM],
        out_specs=(VMEM, VMEM),
        scratch_shapes=[pltpu.VMEM((children * rows, width), jnp.bfloat16)] * 2
        + [pltpu.VMEM(mine.shape, F32)],
        compiler_params=PARAMS,
        name="add_children",
    )(parent, mine, arrived)


def row8(x, i):
    return jnp.broadcast_to(x[i : i + 1, :], (8, LB))


def lane8(x, j):
    return jnp.broadcast_to(x[:, j : j + 1], (8, LB))


def total8(terms):
    while len(terms) > 1:
        terms = [terms[i] + terms[i + 1] for i in range(0, len(terms), 2)]
    return terms[0]


def factor_block(slabs):
    count, panel, ahead = len(slabs), 4, 2
    sub = lax.broadcasted_iota(jnp.int32, (8, LB), 0)
    lane = lax.broadcasted_iota(jnp.int32, (8, LB), 1)
    slabs = list(slabs)
    r_out, inv_out = [], []
    here = [jnp.maximum(lane8(slabs[0], j), F32(-3e38)) for j in range(8)]
    for p in range(0, count, panel):
        end = p + panel
        reach = min(end + ahead, count)
        for b in range(p, end):
            a = [[row8(here[j], i) if i <= j else None for j in range(8)] for i in range(8)]
            row = sub + 8 * b
            joined = slabs[b] + jnp.where(lane == row, F32(1), F32(0))
            r = [row8(joined, i) for i in range(8)]
            rd = [None] * 8
            m = [[None] * 8 for _ in range(8)]
            vectors = [r]
            if b + 1 < reach:
                c = [lane8(slabs[b + 1], 8 * b + j) for j in range(8)]
                here = [lane8(slabs[b + 1], 8 * (b + 1) + j) for j in range(8)]
                vectors.append(c)
            for k in range(8):
                rd[k] = 1.0 / a[k][k]
                for j in range(k + 1, 8):
                    m[k][j] = a[k][j] * rd[k]
                    for i in range(j, 8):
                        a[j][i] = a[j][i] - m[k][j] * a[k][i]
                    for vector in vectors:
                        vector[j] = vector[j] - m[k][j] * vector[k]
            pivots, rows = a[0][0], r[0]
            for k in range(1, 8):
                pivots = jnp.where(sub == k, a[k][k], pivots)
                rows = jnp.where(sub == k, r[k], rows)
            rs = lax.rsqrt(pivots)
            rows = rows * rs
            r_out.append(
                jnp.where(lane > row, rows, jnp.where(lane == row, pivots * rs, F32(0)))
            )
            inv_out.append(jnp.where(lane < row, rows, jnp.where(lane == row, rs, F32(0))))
            if b + 1 == reach:
                continue
            u = [c[j] * rd[j] for j in range(8)]
            for j in range(8):
                slabs[b + 1] = slabs[b + 1] - u[j] * r[j]
            for j in range(8):
                for k in range(8):
                    here[j] = here[j] - u[k] * row8(c[k], j)
            if b + 2 == reach:
                continue
            z = [None] * 8
            for k in reversed(range(8)):
                z[k] = r[k] * rd[k]
                for i in range(k + 1, 8):
                    z[k] = z[k] - m[k][i] * z[i]
            for v in range(b + 2, reach):
                cv = [lane8(slabs[v], 8 * b + j) for j in range(8)]
                slabs[v] = slabs[v] - total8([cv[j] * z[j] for j in range(8)])
        if reach < count:
            both = [jnp.where(lane >= 8 * end, r_out[v], inv_out[v]) for v in range(p, end)]
            hi, lo = split(jnp.concatenate(both, axis=0))
            taken = dot(
                jnp.concatenate([hi, hi, lo], axis=0), jnp.concatenate([hi, lo, hi], axis=0), TN
            )
            dead = (lane >= 8 * p) & (lane < 8 * end)
            for v in range(reach, count):
                slabs[v] = jnp.where(dead, F32(0), slabs[v]) - taken[8 * v : 8 * v + 8, :]
    return r_out, inv_out


def tall(a, axis):
    return jnp.concatenate([a[0], a[0], a[1]], axis=axis)


def wide(b, axis):
    return jnp.concatenate([b[0], b[1], b[0]], axis=axis)


def product(a, b, dims):
    return dot(tall(a, dims[0][0]), wide(b, dims[1][0]), dims)


def factor_kernel(
    total_rows, live_ref, mine_ref, other_ref, own_ref, r_ref, q_ref,
    a_ref, inv_ref, strip_ref, q_now_ref,
):
    local, width = own_ref.shape
    n = width // LB
    half = mine_ref.shape[0]
    place = lax.axis_index("rows")
    core, chip = place % 2, place // 2
    diag = lax.broadcasted_iota(jnp.int32, (LB, LB), 0) == lax.broadcasted_iota(
        jnp.int32, (LB, LB), 1
    )
    blocks = upper_blocks(width)

    def fetch(at):
        side, rows = packed_rows(at, chip, half)
        parts = [
            jnp.where(
                core == side, mine_ref[pl.ds(o, LB // 2), :], other_ref[pl.ds(o, LB // 2), :]
            )
            for o in rows
        ]
        return jnp.concatenate(parts, axis=0)

    across, down = [], []
    for i in range(n):
        only = jnp.where(diag, fetch(blocks.index((i, i))), F32(0))
        across.append(
            lax.rsqrt(jnp.sum(only, axis=0, keepdims=True) / total_rows + F32(1e-6))
        )
        down.append(lax.rsqrt(jnp.sum(only, axis=1, keepdims=True) / total_rows + F32(1e-6)))
    root = 2.0 ** ((total_rows.bit_length() - 1) // 2)
    down = [x * F32(1 / root**2) for x in down]
    shift = jnp.where(diag, F32(0.25 * total_rows / root**2), F32(0))

    def scaled(at):
        i, j = blocks[at]
        block = fetch(at) * down[i] * across[j]
        return block + shift if i == j else block

    def unpack():
        for at, (i, j) in enumerate(blocks):
            if at > 0:
                a_ref[i * LB : (i + 1) * LB, j * LB : (j + 1) * LB] = scaled(at)
        rows = lax.broadcasted_iota(jnp.int32, (local, LB), 0)
        live = live_here(live_ref, local)
        for j in range(n):
            cols = slice(j * LB, (j + 1) * LB)
            q_ref[:, cols] = jnp.where(
                rows < live, own_ref[:, cols] * (across[j] * F32(1 / root)), F32(0)
            )

    def take_strip(first):
        left = first * LB
        old = split(strip_ref[...])
        old_tall, old_wide = tall(old, 0), wide(old, 0)
        for i in range(first, n):
            at = slice(i * LB, (i + 1) * LB)
            a_ref[at, i * LB :] = a_ref[at, i * LB :] - dot(
                old_tall[:, at], old_wide[:, i * LB :], TN
            )
        q_ref[:, left:] = q_ref[:, left:] - dot(
            tall(split(q_now_ref[...]), 1), old_wide[:, left:], NN
        )

    def step(first, k, carry):
        o = pl.multiple_of(k * LB, LB)
        if first is None:
            left = 0
            block = scaled(0)
            slabs = [block[8 * v : 8 * v + 8, :] for v in range(LB // 8)]
            unpack()
        else:
            left = first * LB
            slabs = [a_ref[pl.ds(o + 8 * v, 8), pl.ds(o, LB)] for v in range(LB // 8)]
            take_strip(first)
        r_rows, inv_rows = factor_block(slabs)
        for v in range(LB // 8):
            inv_ref[8 * v : 8 * v + 8, :] = inv_rows[v]
        inv = split(inv_ref[...])
        strip = product(inv, split(a_ref[pl.ds(o, LB), left:]), NN)
        column = lax.broadcasted_iota(jnp.int32, strip.shape, 1) + left
        strip = jnp.where(column >= o + LB, strip, F32(0))
        strip_ref[:, left:] = strip
        a_ref[pl.ds(o, LB), left:] = strip
        for v in range(LB // 8):
            a_ref[pl.ds(o + 8 * v, 8), pl.ds(o, LB)] = r_rows[v]
        after = pl.multiple_of(jnp.minimum(k + 1, n - 1) * LB, LB)
        new = split(strip_ref[:, pl.ds(after, LB)])
        a_ref[pl.ds(after, LB), pl.ds(after, LB)] = a_ref[
            pl.ds(after, LB), pl.ds(after, LB)
        ] - product(new, new, TN)
        q_now = product(split(q_ref[:, pl.ds(o, LB)]), inv, NT)
        q_now_ref[...] = q_now
        q_ref[:, pl.ds(o, LB)] = q_now
        return carry

    step(None, jnp.int32(0), 0)
    for first, last in ((1, 3), (3, 5), (5, n)):
        lax.fori_loop(first, last, functools.partial(step, first), 0)
    start = pl.multiple_of(place * r_ref.shape[0], r_ref.shape[0])
    mine = a_ref[pl.ds(start, r_ref.shape[0]), :]
    row = start + lax.broadcasted_iota(jnp.int32, mine.shape, 0)
    column = lax.broadcasted_iota(jnp.int32, mine.shape, 1)
    r_ref[...] = jnp.where(column >= row, mine * F32(root), F32(0))


def factor(live_rows, mine, other, own, out_rows, total_rows):
    local, width = own.shape
    return pl.pallas_call(
        functools.partial(factor_kernel, total_rows),
        out_shape=(
            jax.ShapeDtypeStruct((out_rows, width), F32),
            jax.ShapeDtypeStruct(own.shape, F32),
        ),
        in_specs=[SMEM, VMEM, VMEM, VMEM],
        out_specs=(VMEM, VMEM),
        scratch_shapes=[
            pltpu.VMEM((width, width), F32),
            pltpu.VMEM((LB, LB), F32),
            pltpu.VMEM((LB, width), F32),
            pltpu.VMEM((local, LB), F32),
        ],
        compiler_params=PARAMS,
        name="factor",
    )(live_rows, mine, other, own)


def to_chip(x, k):
    devices = lax.axis_size("rows")
    pairs = [(i, (i + (2 * k if i % 2 == 0 else -2 * k)) % devices) for i in range(devices)]
    return lax.ppermute(x, "rows", pairs)


def to_core(x):
    return lax.ppermute(x, "rows", [(i, i ^ 1) for i in range(lax.axis_size("rows"))])


def sum_over_rows(keep, send):
    chips = lax.axis_size("rows") // 2
    classes = [
        [2 * (a + 4 * i) + c for i in range(chips // 4)] for c in range(2) for a in range(4)
    ]
    quarter = keep.shape[0] // 4
    got = to_core(send)
    part = [
        keep[k * quarter : (k + 1) * quarter] + got[k * quarter : (k + 1) * quarter]
        for k in range(4)
    ]
    far = to_chip(part[2], -2)
    summed = part[0] + to_chip(part[1], 1) + to_chip(part[3], -1) + far
    pieces = lax.all_to_all(
        summed, "rows", split_axis=0, concat_axis=0, axis_index_groups=classes, tiled=True
    )
    done = jnp.sum(pieces.reshape(chips // 4, -1, LB), axis=0)
    whole = lax.all_gather(done, "rows", axis=0, axis_index_groups=classes, tiled=True)
    right = to_chip(whole, -1)
    left = to_chip(whole, 1)
    far = to_chip(whole, -2)
    mine = jnp.concatenate([whole, right, far, left])
    return mine, to_core(mine)


def body(own_rows, child_tile, col_map, parent, live_rows):
    own, tile = own_rows[0], child_tile[0]
    arrived = lax.all_to_all(
        place_child(parent, tile, col_map), "front", split_axis=0, concat_axis=0, tiled=True
    )
    keep, send = add_children(parent, own_gram(live_rows, own), arrived)
    mine, other = sum_over_rows(keep, send)
    total_rows = own.shape[0] * lax.axis_size("rows")
    r_rows, panel = factor(live_rows, mine, other, own, tile.shape[0], total_rows)
    return (r_rows[None], panel[None])


def solution(mesh):
    placed = (P("front", "rows", None), P("front", "rows", None), P(), P(), P())
    return jax.shard_map(
        body,
        mesh=mesh,
        in_specs=placed,
        out_specs=(P("front", "rows", None), P("front", "rows", None)),
        check_vma=False,
    )
```
